256 devices in a mesh: req: 1, span: 32 (over y, x, core), head: 8 (over z).
Axes of the slice: x: 4, y: 4, z: 8, core: 2. Of those that a mesh axis runs over, the one named last changes fastest.
Arguments:
- hidden_rows: bfloat16 [32, 128, 8192], P(('req', 'span')), may hold values from -6 to 6
- w_query: bfloat16 [8192, 4096], P('span', 'head'), may hold values from -0.0625 to 0.0625
- w_key: bfloat16 [8192, 1024], P('span', 'head'), may hold values from -0.0625 to 0.0625
- w_value: bfloat16 [8192, 1024], P('span', 'head'), may hold values from -0.0625 to 0.0625
- cache_keys: bfloat16 [32, 1024, 1024], P(('req', 'span'), None, 'head'), may hold values from -4 to 4
- cache_values: bfloat16 [32, 1024, 1024], P(('req', 'span'), None, 'head'), may hold values from -4 to 4
- key_scale: float32 [32, 8, 1024], P(('req', 'span'), 'head'), may hold values from 0.5 to 240
- value_scale: float32 [32, 8, 1024], P(('req', 'span'), 'head'), may hold values from 0.5 to 2
- sel_index: int32 [32, 128], P(('req', 'span')), may hold values from 0 to 1023, as said below
- sel_count: int32 [32], P(('req', 'span')), may hold values from 64 to 128, as said below
Outputs:
- attended: bfloat16 [32, 128, 4096], P(('req', 'span'), None, 'head')
- blend_keys: bfloat16 [32, 1024, 1024], P(('req', 'span'), None, 'head')
- blend_values: bfloat16 [32, 1024, 1024], P(('req', 'span'), None, 'head')
The draws below stay inside these ranges and needn't reach their ends.
Inputs may be any that keep to these rules, and one draw needn't show every extreme that they name: `sel_index`: within one span the 128 entries are distinct positions; only the first sel_count entries are used. `sel_count`: some span uses all 128 slots.
All inputs are finite; a program needn't handle non-finite values.
Results may differ from the reference program's by a relative error of at most 0.022.
The reference program's roundings to bfloat16 on the way (of `queries`, `dequantized` and `weights`) count: a program that leaves them out, or rounds other values in their place, can miss the bound.
Values may be sent and summed in bfloat16 or wider, within the bound.
A program may use at most 128 MiB of HBM per device.

```python
import math
import jax
import jax.numpy as jnp
from jax import lax

D = 8192
HEAD_DIM = 128
KV_HEADS = 8
GROUP = 4
SPAN_LEN = 1024
SEL = 128
SPANS = 32


def draw_key_scale(key, part):
    key = jax.random.fold_in(key, 11)
    base_key = jax.random.fold_in(key, 0)
    shape = (SPANS, KV_HEADS, SPAN_LEN)
    scales = jnp.exp(jax.random.uniform(base_key, shape, jnp.float32, jnp.log(0.5), jnp.log(2.0)))
    return scales.astype(jnp.float32)


def draw_sel_index(key, part):
    key = jax.random.fold_in(key, 23)
    span_keys = jax.random.split(key, SPANS)
    rows = jax.vmap(lambda one_key: jax.random.permutation(one_key, SPAN_LEN)[:SEL])(span_keys)
    return rows.astype(jnp.int32)


def draw_sel_count(key, part):
    key = jax.random.fold_in(key, 37)
    count_key, full_key = jax.random.split(key)
    counts = jax.random.randint(count_key, (SPANS,), SEL // 2, SEL + 1)
    full_span = jax.random.randint(full_key, (), 0, SPANS)
    counts = counts.at[full_span].set(SEL)
    return counts.astype(jnp.int32)


def block_scale(rng, dims, cuts, smallest, top_value):
    gain, own = 1.0, jax.random.fold_in(rng, 6)
    for axis_at, parts in cuts:
        steps = jnp.exp(jax.random.uniform(jax.random.fold_in(own, axis_at), (parts,), jnp.float32, smallest / len(cuts), top_value / len(cuts)))
        gain = gain * jnp.repeat(steps, dims[axis_at] // parts).reshape([-1 if axis == axis_at else 1 for axis in range(len(dims))])
    return gain


def normal_values(own_key, dims, scale, reach, cuts=(), held_as=jnp.bfloat16):
    drawn = jax.random.normal(own_key, dims, jnp.float32) * scale
    if len(cuts) > 0:
        drawn = block_scale(own_key, dims, cuts, -0.22, 0.18) * drawn
    return jnp.clip(drawn, min=-reach, max=reach).astype(held_as)


def setup_inputs(seed: int = 0, part: int = 0) -> dict:
    keys = jax.random.split(jax.random.key(seed), 11)
    part_keys = jax.random.split(jax.random.fold_in(keys[10], part), 11)
    hidden_rows = normal_values(part_keys[0], (SPANS, SEL, D), 1.0, 6.0, ((0, 32),))
    w_query = normal_values(keys[1], (D, KV_HEADS * GROUP * HEAD_DIM), D ** -0.5, 0.0625, ((0, 32), (1, 8)))
    w_key = normal_values(keys[2], (D, KV_HEADS * HEAD_DIM), D ** -0.5, 0.0625, ((0, 32), (1, 8)))
    w_value = normal_values(keys[3], (D, KV_HEADS * HEAD_DIM), D ** -0.5, 0.0625, ((0, 32), (1, 8)))
    cache_keys = normal_values(part_keys[4], (SPANS, SPAN_LEN, KV_HEADS * HEAD_DIM), 1.0, 4.0, ((0, 32), (2, 8)))
    cache_values = normal_values(part_keys[5], (SPANS, SPAN_LEN, KV_HEADS * HEAD_DIM), 1.0, 4.0, ((0, 32), (2, 8)))
    key_scale = draw_key_scale(jax.random.fold_in(jax.random.fold_in(keys[10], part), 71), part)
    value_scale = jnp.clip(jnp.exp(math.log(2.0) - 1.3862944 * jax.random.uniform(part_keys[7], (SPANS, KV_HEADS, SPAN_LEN), jnp.float32) ** block_scale(part_keys[7], (SPANS, KV_HEADS, SPAN_LEN), ((0, 32), (1, 8)), -0.2, 0.2)), 0.5, 2.0)
    sel_index = draw_sel_index(jax.random.fold_in(jax.random.fold_in(keys[10], part), 71), part)
    sel_count = draw_sel_count(jax.random.fold_in(jax.random.fold_in(keys[10], part), 71), part)
    return dict(hidden_rows=hidden_rows, w_query=w_query, w_key=w_key, w_value=w_value, cache_keys=cache_keys, cache_values=cache_values, key_scale=key_scale, value_scale=value_scale, sel_index=sel_index, sel_count=sel_count)


def blend(cache_rows, scale_rows, fresh_rows, target):
    dequantized = (cache_rows.astype(jnp.float32).reshape(SPANS, SPAN_LEN, KV_HEADS, HEAD_DIM) * jnp.transpose(scale_rows, (0, 2, 1))[..., None]).reshape(SPANS, SPAN_LEN, KV_HEADS * HEAD_DIM).astype(jnp.bfloat16)
    return jax.vmap(lambda base, where_to, rows: base.at[where_to].set(rows, mode="drop"))(dequantized, target, fresh_rows)


def reference(hidden_rows, w_query, w_key, w_value, cache_keys, cache_values, key_scale, value_scale, sel_index, sel_count):
    flat = hidden_rows.reshape(SPANS * SEL, D)
    queries = jnp.dot(flat, w_query, preferred_element_type=jnp.float32).astype(jnp.bfloat16).reshape(SPANS, SEL, KV_HEADS, GROUP, HEAD_DIM)
    new_keys = jnp.dot(flat, w_key, preferred_element_type=jnp.float32).astype(jnp.bfloat16).reshape(SPANS, SEL, KV_HEADS * HEAD_DIM)
    new_values = jnp.dot(flat, w_value, preferred_element_type=jnp.float32).astype(jnp.bfloat16).reshape(SPANS, SEL, KV_HEADS * HEAD_DIM)
    valid = jnp.arange(SEL, dtype=jnp.int32)[None, :] < sel_count[:, None]
    target = jnp.where(valid, sel_index, SPAN_LEN).astype(jnp.int32)
    blend_keys = blend(cache_keys, key_scale, new_keys, target)
    blend_values = blend(cache_values, value_scale, new_values, target)
    all_keys = blend_keys.reshape(SPANS * SPAN_LEN, KV_HEADS, HEAD_DIM).astype(jnp.float32)
    all_values = blend_values.reshape(SPANS * SPAN_LEN, KV_HEADS, HEAD_DIM).astype(jnp.float32)
    key_pos = jnp.arange(SPANS * SPAN_LEN, dtype=jnp.int32)
    query_pos = (jnp.arange(SPANS, dtype=jnp.int32)[:, None] * SPAN_LEN + sel_index).astype(jnp.int32)

    def one_span(inputs):
        span_queries, span_pos = inputs
        scores = jnp.einsum("shgd,khd->shgk", span_queries.astype(jnp.float32), all_keys) * (HEAD_DIM ** -0.5)
        allowed = (key_pos[None, :] <= span_pos[:, None])[:, None, None, :]
        scores = jnp.where(allowed, scores, -1e30)
        largest = jnp.max(scores, axis=-1, keepdims=True)
        weights = jnp.where(allowed, jnp.exp(scores - largest), 0.0)
        total = jnp.sum(weights, axis=-1)
        rounded = lax.optimization_barrier(weights.astype(jnp.bfloat16))
        summed = jnp.einsum("shgk,khd->shgd", rounded.astype(jnp.float32), all_values)
        return summed / total[..., None]

    attended = lax.map(one_span, (queries, query_pos))
    attended = jnp.where(valid[:, :, None, None, None], attended, 0.0)
    attended = attended.reshape(SPANS, SEL, KV_HEADS * GROUP * HEAD_DIM).astype(jnp.bfloat16)
    return attended, blend_keys, blend_values
```

```python
import math

import jax
import jax.numpy as jnp
from jax import lax
from jax.experimental import pallas as pl
from jax.experimental.pallas import tpu as pltpu
from jax.sharding import PartitionSpec as P

HEAD_DIM = 128
GROUP = 4
SLOTS = 128
SPAN_LEN = 1024
SIDE = 4
CHIPS = SIDE * SIDE
DEPTH = 256
ROWS = GROUP * SLOTS
KEYS = 2 * SPAN_LEN
EXP2_SCALE = math.log2(math.e) / math.sqrt(HEAD_DIM)
F32 = jnp.float32
BF16 = jnp.bfloat16
OFFSETS = (0, -1, 1, 2)


def position():
    span = lax.axis_index("span")
    core = lax.rem(span, 2)
    chip = lax.div(span, 2)
    return chip, core


def device_of(chip, core):
    return {"span": chip * 2 + core}


class Gather:
    def __init__(self, buf, rows, chip, core, send_sem, recv_sem):
        self.buf, self.rows, self.chip, self.core = buf, rows, chip, core
        self.send_sem, self.recv_sem = send_sem, recv_sem
        self.at = (lax.rem(chip, SIDE), lax.div(chip, SIDE))
        self.sent = []

    def block(self, dx, dy):
        x = lax.rem(self.at[0] + (dx + SIDE), SIDE)
        y = lax.rem(self.at[1] + (dy + SIDE), SIDE)
        return y * SIDE + x

    def along(self, axis, first, second):
        return self.block(first, second) if axis == 0 else self.block(second, first)

    def piece(self, half, block, kind):
        size = self.rows // 2
        start = half * size
        if kind >= 2:
            size //= 2
            start += (kind - 2) * size
        return self.buf.at[block, pl.ds(start, size), :]

    def copy(self, half, stage, j, kind, block, target):
        where = half * 20 + (kind if stage == 1 else 4 + j * 4 + kind)
        ref = self.piece(half, block, kind)
        return pltpu.make_async_remote_copy(
            src_ref=ref,
            dst_ref=ref,
            send_sem=self.send_sem.at[where],
            recv_sem=self.recv_sem.at[where],
            device_id=device_of(target, self.core),
            device_id_type=pl.DeviceIdType.MESH,
        )

    def locate(self, half, stage, j, shift):
        if stage == 1:
            return self.along(half, shift, 0)
        return self.along(half, OFFSETS[j], shift)

    def step(self, half, stage, way):
        axis = half if stage == 1 else 1 - half
        return self.along(axis, way, 0)

    def send(self, half, stage, j, kind, shift):
        way = 1 if kind % 2 == 0 else -1
        one = self.copy(half, stage, j, kind, self.locate(half, stage, j, shift), self.step(half, stage, way))
        one.start()
        self.sent.append(one)

    def receive(self, half, stage, j, kind):
        shift = (-1, 1, 2, 2)[kind]
        self.copy(half, stage, j, kind, self.locate(half, stage, j, shift), self.chip).wait_recv()

    def spread(self, half, stage, j):
        self.send(half, stage, j, 0, 0)
        self.send(half, stage, j, 1, 0)

    def begin(self):
        for half in (0, 1):
            self.spread(half, 1, 0)
        for half in (0, 1):
            self.spread(half, 2, 0)

    def fulls(self, stage, j):
        for kind in (0, 1):
            for half in (0, 1):
                self.receive(half, stage, j, kind)
                self.send(half, stage, j, kind + 2, (-1, 1)[kind])
                if stage == 1:
                    self.spread(half, 2, 1 + kind)

    def quarters(self, stage, j):
        for half in (0, 1):
            for kind in (2, 3):
                self.receive(half, stage, j, kind)
            if stage == 1:
                self.spread(half, 2, 3)

    def finish(self):
        for one in self.sent:
            one.wait_send()


def project(acc, hid_v, buf, block, first=False):
    part = jnp.dot(hid_v[block], buf[block], preferred_element_type=F32)
    acc[...] = part if first else acc[...] + part


def run_gather(gather, acc, hid_v, buf, first_work):
    def work(*pairs):
        for dx, dy in pairs:
            project(acc, hid_v, buf, gather.block(dx, dy))

    first_work()
    gather.fulls(1, 0)
    gather.fulls(2, 0)
    work((-1, 0), (1, 0), (0, -1), (0, 1))
    gather.quarters(1, 0)
    gather.fulls(2, 1)
    gather.fulls(2, 2)
    work((-1, -1), (1, -1), (-1, 1), (1, 1))
    gather.quarters(2, 0)
    work((2, 0), (0, 2))
    gather.fulls(2, 3)
    gather.quarters(2, 1)
    gather.quarters(2, 2)
    work((2, -1), (2, 1), (-1, 2), (1, 2))
    gather.quarters(2, 3)
    work((2, 2))


def body(
    hid, wq, wk, wv, ck, cv, ks, vs, sel, cnt,
    att_o, bk_o, bv_o,
    hid_v, wkv_buf, wq_buf, acc_kv, acc_q, pkv_in, pq_in, cache_v, kbuf, vbuf,
    qbuf, osend, res, stat, stat_t, stat_in, out_acc, att_v,
    local_sem, out_sem, hid_sem, part_sem, kv_sem,
    akv_send, akv_recv, aq_send, aq_recv,
    q_send, q_recv, r_send, r_recv, s_send, s_recv,
):
    chip, core = position()
    sibling = device_of(chip, 1 - core)

    def remote(src, dst, send_sem, recv_sem, device):
        return pltpu.make_async_remote_copy(
            src_ref=src, dst_ref=dst, send_sem=send_sem, recv_sem=recv_sem,
            device_id=device, device_id_type=pl.DeviceIdType.MESH,
        )

    barrier = pltpu.get_barrier_semaphore()
    pl.semaphore_signal(barrier, inc=1, device_id=sibling, device_id_type=pl.DeviceIdType.MESH)

    def greet(step, carry):
        other = lax.rem(chip + step, CHIPS)
        pl.semaphore_signal(
            barrier, inc=1, device_id=device_of(other, core), device_id_type=pl.DeviceIdType.MESH
        )
        return carry

    lax.fori_loop(1, CHIPS, greet, 0)

    loads = [
        pltpu.make_async_copy(wk, wkv_buf.at[chip, :, pl.ds(0, HEAD_DIM)], local_sem.at[0]),
        pltpu.make_async_copy(wv, wkv_buf.at[chip, :, pl.ds(HEAD_DIM, HEAD_DIM)], local_sem.at[1]),
        pltpu.make_async_copy(wq, wq_buf.at[chip], local_sem.at[2]),
        pltpu.make_async_copy(ck.at[0], cache_v.at[0], local_sem.at[3]),
        pltpu.make_async_copy(cv.at[0], cache_v.at[1], local_sem.at[4]),
    ]
    for one in loads:
        one.start()

    def load_hidden(block, carry):
        start = pl.multiple_of((block * 2 + core) * DEPTH, DEPTH)
        pltpu.make_async_copy(
            hid.at[0, :, pl.ds(start, DEPTH)], hid_v.at[block, pl.ds(0, SLOTS), :], local_sem.at[5]
        ).start()
        return carry

    lax.fori_loop(0, CHIPS, load_hidden, 0)
    pl.semaphore_wait(barrier, CHIPS)

    gkv = Gather(wkv_buf, DEPTH, chip, core, akv_send, akv_recv)
    gq = Gather(wq_buf, DEPTH, chip, core, aq_send, aq_recv)
    loads[0].wait()
    loads[1].wait()
    gkv.begin()
    loads[2].wait()
    gq.begin()

    def send_hidden(block, carry):
        start = pl.multiple_of((block * 2 + 1 - core) * DEPTH, DEPTH)
        remote(
            hid.at[0, :, pl.ds(start, DEPTH)], hid_v.at[block, pl.ds(SLOTS, SLOTS), :],
            hid_sem.at[0], hid_sem.at[1], sibling,
        ).start()
        return carry

    lax.fori_loop(0, CHIPS, send_hidden, 0)
    hid_own = hid_v.at[:, pl.ds(0, SLOTS), :]
    hid_far = hid_v.at[:, pl.ds(SLOTS, SLOTS), :]
    hid_copy = remote(hid_far, hid_far, hid_sem.at[0], hid_sem.at[1], sibling)

    loads[3].wait()
    loads[4].wait()
    own_keys = pl.multiple_of(core * SPAN_LEN, SPAN_LEN)
    for which, (scale, target) in enumerate(((ks, kbuf), (vs, vbuf))):
        for part in range(SPAN_LEN // 128):
            row = scale[0, :, part * 128:(part + 1) * 128]
            spread = jnp.transpose(jnp.broadcast_to(row, (128, 128)))
            codes = cache_v[which, part * 128:(part + 1) * 128, :].astype(F32)
            target[pl.ds(own_keys + part * 128, 128), :] = (codes * spread).astype(BF16)

    def first_kv():
        pltpu.make_async_copy(hid_own, hid_own, local_sem.at[5]).wait()
        hid_copy.wait_recv()
        project(acc_kv, hid_v, wkv_buf, chip, first=True)
        project(acc_q, hid_v, wq_buf, chip, first=True)

    run_gather(gkv, acc_kv, hid_v, wkv_buf, first_kv)
    kv_part = remote(
        acc_kv.at[pl.ds(SLOTS, SLOTS), :], pkv_in, part_sem.at[0], part_sem.at[1], sibling
    )
    kv_part.start()

    slot_row = lax.broadcasted_iota(jnp.int32, (1, SLOTS), 1)
    count = cnt[0]
    wanted = jnp.where(slot_row < count, sel[...], -1)

    def blend():
        kv_part.wait_recv()
        fresh = (acc_kv[0:SLOTS, :] + pkv_in[...]).astype(BF16)
        ones = jnp.ones((SLOTS, HEAD_DIM), BF16)

        def part(step, carry):
            start = pl.multiple_of(step * 128, 128)
            rows = lax.broadcasted_iota(jnp.int32, (128, SLOTS), 0) + start
            chosen = jnp.where(rows == wanted, 1.0, 0.0).astype(BF16)
            moved = jnp.dot(chosen, fresh, preferred_element_type=F32)
            hit = jnp.dot(chosen, ones, preferred_element_type=F32) > 0.5
            here = pl.ds(pl.multiple_of(own_keys + start, 128), 128)
            kbuf[here, :] = jnp.where(hit, moved[:, :HEAD_DIM], kbuf[here, :].astype(F32)).astype(BF16)
            vbuf[here, :] = jnp.where(hit, moved[:, HEAD_DIM:], vbuf[here, :].astype(F32)).astype(BF16)
            return carry

        lax.fori_loop(0, SPAN_LEN // 128, part, 0)

    own_span = pl.ds(own_keys, SPAN_LEN)
    k_copy = remote(kbuf.at[own_span, :], kbuf.at[own_span, :], kv_sem.at[0], kv_sem.at[1], sibling)
    v_copy = remote(vbuf.at[own_span, :], vbuf.at[own_span, :], kv_sem.at[2], kv_sem.at[3], sibling)
    k_out = pltpu.make_async_copy(kbuf.at[own_span, :], bk_o.at[0], out_sem.at[0])
    v_out = pltpu.make_async_copy(vbuf.at[own_span, :], bv_o.at[0], out_sem.at[1])

    def start_kv():
        blend()
        for one in (k_copy, v_copy, k_out, v_out):
            one.start()

    run_gather(gq, acc_q, hid_v, wq_buf, start_kv)
    q_part = remote(acc_q.at[pl.ds(SLOTS, SLOTS), :], pq_in, part_sem.at[2], part_sem.at[3], sibling)
    q_part.start()
    other_keys = pl.multiple_of((1 - core) * SPAN_LEN, SPAN_LEN)
    other_span = pl.ds(other_keys, SPAN_LEN)
    remote(kbuf.at[other_span, :], kbuf.at[other_span, :], kv_sem.at[0], kv_sem.at[1], sibling).wait_recv()
    remote(vbuf.at[other_span, :], vbuf.at[other_span, :], kv_sem.at[2], kv_sem.at[3], sibling).wait_recv()
    stat[...] = jnp.zeros((ROWS, 128), F32)
    q_part.wait_recv()
    for g in range(GROUP):
        cols = slice(g * HEAD_DIM, (g + 1) * HEAD_DIM)
        qbuf[chip, cols, :] = (acc_q[0:SLOTS, cols] + pq_in[:, cols]).astype(BF16)

    def q_copy(source, target):
        return remote(
            qbuf.at[source], qbuf.at[source], q_send.at[target], q_recv.at[source],
            device_of(target, core),
        )

    def send_q(target, carry):
        q_copy(chip, target).start()
        return carry

    lax.fori_loop(0, chip, send_q, 0)

    lane = lax.broadcasted_iota(jnp.int32, (256, 128), 1)

    def attend(source, half, store, limit):
        here = pl.ds(pl.multiple_of(half * 256, 256), 256)
        scores = lax.dot_general(
            qbuf[source, here, :], kbuf[...], (((1,), (1,)), ((), ())), preferred_element_type=F32
        )
        if limit is not None:
            key = lax.broadcasted_iota(jnp.int32, (256, KEYS), 1)
            scores = jnp.where(key <= limit, scores, -1e30)
        best = jnp.max(scores, axis=1, keepdims=True)
        weights = jnp.exp2((scores - best) * EXP2_SCALE)
        total = jnp.sum(weights, axis=1, keepdims=True)
        summed = jnp.dot(weights.astype(BF16), vbuf[...], preferred_element_type=F32)
        store[source, here, :] = summed.astype(BF16)
        old = stat[here, :]
        old = jnp.where(lane == source * 8, best, old)
        stat[here, :] = jnp.where(lane == source * 8 + 1, total, old)

    place = jnp.transpose(jnp.broadcast_to(sel[...], (128, 128)))[:, 0:1] + core * SPAN_LEN
    limit = jnp.concatenate([place, place], axis=0)

    def own_half(half, carry):
        attend(chip, half, res, limit)
        return carry

    lax.fori_loop(0, 2, own_half, 0)

    def r_copy(source, target):
        return remote(
            osend.at[target], res.at[source], r_send.at[target], r_recv.at[source],
            device_of(target, core),
        )

    def s_copy(source, target):
        return remote(
            stat_t.at[target], stat_in.at[source], s_send.at[target], s_recv.at[source],
            device_of(target, core),
        )

    def others(source, carry):
        q_copy(source, chip).wait_recv()

        def one_half(half, inner):
            attend(source, half, osend, None)
            return inner

        lax.fori_loop(0, 2, one_half, 0)
        r_copy(chip, source).start()
        return carry

    lax.fori_loop(chip + 1, CHIPS, others, 0)
    stat_t[...] = jnp.transpose(stat[...]).reshape(CHIPS, 8, ROWS)

    def send_stat(target, carry):
        s_copy(chip, target).start()
        return carry

    lax.fori_loop(chip + 1, CHIPS, send_stat, 0)
    stat_in[chip] = stat_t[chip]

    def take(source, carry):
        s_copy(source, chip).wait_recv()
        return carry

    lax.fori_loop(0, chip, take, 0)
    seen = stat_in[...]
    known = lax.broadcasted_iota(jnp.int32, (CHIPS, 1, ROWS), 0) <= chip
    bests = jnp.where(known, seen[:, 0:1, :], -3e38)
    top = jnp.max(bests, axis=0, keepdims=True)
    factor = jnp.where(known, jnp.exp2((bests - top) * EXP2_SCALE), 0.0)
    total = jnp.sum(jnp.where(known, factor * seen[:, 1:2, :], 0.0), axis=0, keepdims=True)
    factor = factor / total
    stat[...] = jnp.transpose(jnp.broadcast_to(factor, (CHIPS, 8, ROWS)).reshape(CHIPS * 8, ROWS))
    out_acc[...] = jnp.zeros((ROWS, HEAD_DIM), F32)

    def add(source):
        wide = lax.broadcasted_iota(jnp.int32, (ROWS, 128), 1)
        weight = jnp.sum(jnp.where(wide == source * 8, stat[...], 0.0), axis=1, keepdims=True)
        out_acc[...] += res[source].astype(F32) * weight

    add(chip)

    def add_far(source, carry):
        r_copy(source, chip).wait_recv()
        add(source)
        return carry

    lax.fori_loop(0, chip, add_far, 0)
    used = lax.broadcasted_iota(jnp.int32, (SLOTS, HEAD_DIM), 0) < count
    for g in range(GROUP):
        cols = slice(g * HEAD_DIM, (g + 1) * HEAD_DIM)
        att_v[:, cols] = jnp.where(used, out_acc[cols, :], 0.0).astype(BF16)
    a_out = pltpu.make_async_copy(att_v, att_o.at[0], out_sem.at[2])
    a_out.start()

    gkv.finish()
    gq.finish()
    hid_copy.wait_send()
    kv_part.wait_send()
    q_part.wait_send()
    k_copy.wait_send()
    v_copy.wait_send()

    def end_q(target, carry):
        q_copy(chip, target).wait_send()
        return carry

    def end_r(target, carry):
        r_copy(chip, target).wait_send()
        s_copy(chip, target).wait_send()
        return carry

    lax.fori_loop(0, chip, end_q, 0)
    lax.fori_loop(chip + 1, CHIPS, end_r, 0)
    for one in (k_out, v_out, a_out):
        one.wait()


def shards(hidden_rows, w_query, w_key, w_value, cache_keys, cache_values, key_scale, value_scale, sel_index, sel_count):
    any_spec = pl.BlockSpec(memory_space=pl.ANY)
    vmem_spec = pl.BlockSpec(memory_space=pltpu.VMEM)
    smem_spec = pl.BlockSpec(memory_space=pltpu.SMEM)
    dma = pltpu.SemaphoreType.DMA
    return pl.pallas_call(
        body,
        out_shape=(
            jax.ShapeDtypeStruct((1, SLOTS, ROWS), BF16),
            jax.ShapeDtypeStruct((1, SPAN_LEN, HEAD_DIM), BF16),
            jax.ShapeDtypeStruct((1, SPAN_LEN, HEAD_DIM), BF16),
        ),
        in_specs=[any_spec] * 6 + [vmem_spec] * 3 + [smem_spec],
        out_specs=(any_spec,) * 3,
        scratch_shapes=[
            pltpu.VMEM((CHIPS, 2 * SLOTS, DEPTH), BF16),
            pltpu.VMEM((CHIPS, DEPTH, 2 * HEAD_DIM), BF16),
            pltpu.VMEM((CHIPS, DEPTH, ROWS), BF16),
            pltpu.VMEM((2 * SLOTS, 2 * HEAD_DIM), F32),
            pltpu.VMEM((2 * SLOTS, ROWS), F32),
            pltpu.VMEM((SLOTS, 2 * HEAD_DIM), F32),
            pltpu.VMEM((SLOTS, ROWS), F32),
            pltpu.VMEM((2, SPAN_LEN, HEAD_DIM), BF16),
            pltpu.VMEM((KEYS, HEAD_DIM), BF16),
            pltpu.VMEM((KEYS, HEAD_DIM), BF16),
            pltpu.VMEM((CHIPS, ROWS, HEAD_DIM), BF16),
            pltpu.VMEM((CHIPS, ROWS, HEAD_DIM), BF16),
            pltpu.VMEM((CHIPS, ROWS, HEAD_DIM), BF16),
            pltpu.VMEM((ROWS, 128), F32),
            pltpu.VMEM((CHIPS, 8, ROWS), F32),
            pltpu.VMEM((CHIPS, 8, ROWS), F32),
            pltpu.VMEM((ROWS, HEAD_DIM), F32),
            pltpu.VMEM((SLOTS, ROWS), BF16),
            dma((6,)), dma((3,)), dma((2,)), dma((4,)), dma((4,)),
            dma((40,)), dma((40,)), dma((40,)), dma((40,)),
            dma((CHIPS,)), dma((CHIPS,)), dma((CHIPS,)), dma((CHIPS,)), dma((CHIPS,)), dma((CHIPS,)),
        ],
        compiler_params=pltpu.CompilerParams(
            collective_id=0, has_side_effects=True, vmem_limit_bytes=48 * 1024 * 1024
        ),
        name="span_attention",
    )(hidden_rows, w_query, w_key, w_value, cache_keys, cache_values, key_scale, value_scale, sel_index, sel_count)


def solution(mesh):
    placed = (
        P(("req", "span"), None, None),
        P("span", "head"),
        P("span", "head"),
        P("span", "head"),
        P(("req", "span"), None, "head"),
        P(("req", "span"), None, "head"),
        P(("req", "span"), "head", None),
        P(("req", "span"), "head", None),
        P(("req", "span"), None),
        P(("req", "span")),
    )
    return jax.shard_map(
        shards,
        mesh=mesh,
        in_specs=placed,
        out_specs=(
            P(("req", "span"), None, "head"),
            P(("req", "span"), None, "head"),
            P(("req", "span"), None, "head"),
        ),
        check_vma=False,
    )
```

```python
import math

import jax
import jax.numpy as jnp
from jax import lax
from jax.experimental import pallas as pl
from jax.experimental.pallas import tpu as pltpu
from jax.sharding import PartitionSpec as P

HEAD_DIM = 128
GROUP = 4
SLOTS = 128
SPAN_LEN = 1024
SIDE = 4
CHIPS = SIDE * SIDE
DEPTH = 256
ROWS = GROUP * SLOTS
KEYS = 2 * SPAN_LEN
EXP2_SCALE = math.log2(math.e) / math.sqrt(HEAD_DIM)
F32 = jnp.float32
BF16 = jnp.bfloat16
OFFSETS = (0, -1, 1, 2)


def position():
    span = lax.axis_index("span")
    core = lax.rem(span, 2)
    chip = lax.div(span, 2)
    return chip, core


def device_of(chip, core):
    return {"span": chip * 2 + core}


class Gather:
    def __init__(self, buf, first, rows, chip, core, send_sem, recv_sem):
        self.buf, self.first, self.rows, self.chip, self.core = buf, first, rows, chip, core
        self.send_sem, self.recv_sem = send_sem, recv_sem
        self.at = (lax.rem(chip, SIDE), lax.div(chip, SIDE))
        self.sent = []

    def block(self, dx, dy):
        x = lax.rem(self.at[0] + (dx + SIDE), SIDE)
        y = lax.rem(self.at[1] + (dy + SIDE), SIDE)
        return y * SIDE + x

    def along(self, axis, first, second):
        return self.block(first, second) if axis == 0 else self.block(second, first)

    def piece(self, half, block, kind):
        size = self.first if half == 0 else self.rows - self.first
        start = half * self.first
        if kind >= 2:
            size //= 2
            start += (kind - 2) * size
        return self.buf.at[block, pl.ds(start, size), :]

    def copy(self, half, stage, j, kind, block, target):
        where = half * 20 + (kind if stage == 1 else 4 + j * 4 + kind)
        ref = self.piece(half, block, kind)
        return pltpu.make_async_remote_copy(
            src_ref=ref,
            dst_ref=ref,
            send_sem=self.send_sem.at[where],
            recv_sem=self.recv_sem.at[where],
            device_id=device_of(target, self.core),
            device_id_type=pl.DeviceIdType.MESH,
        )

    def locate(self, half, stage, j, shift):
        if stage == 1:
            return self.along(half, shift, 0)
        return self.along(half, OFFSETS[j], shift)

    def step(self, half, stage, way):
        axis = half if stage == 1 else 1 - half
        return self.along(axis, way, 0)

    def send(self, half, stage, j, kind, shift):
        way = 1 if kind % 2 == 0 else -1
        one = self.copy(half, stage, j, kind, self.locate(half, stage, j, shift), self.step(half, stage, way))
        one.start()
        self.sent.append(one)

    def receive(self, half, stage, j, kind):
        shift = (-1, 1, 2, 2)[kind]
        self.copy(half, stage, j, kind, self.locate(half, stage, j, shift), self.chip).wait_recv()

    def spread(self, half, stage, j):
        self.send(half, stage, j, 0, 0)
        self.send(half, stage, j, 1, 0)

    def begin(self):
        for half in (0, 1):
            self.spread(half, 1, 0)
        for half in (0, 1):
            self.spread(half, 2, 0)

    def fulls(self, stage, j):
        for kind in (0, 1):
            for half in (0, 1):
                self.receive(half, stage, j, kind)
                self.send(half, stage, j, kind + 2, (-1, 1)[kind])
                if stage == 1:
                    self.spread(half, 2, 1 + kind)

    def quarters(self, stage, j):
        for half in (0, 1):
            for kind in (2, 3):
                self.receive(half, stage, j, kind)
            if stage == 1:
                self.spread(half, 2, 3)

    def finish(self):
        for one in self.sent:
            one.wait_send()


class Ring:
    def __init__(self, refs, whole, at, device, send_sem, recv_sem):
        self.refs, self.whole, self.at, self.device = refs, whole, at, device
        self.send_sem, self.recv_sem = send_sem, recv_sem
        self.sent = []

    def place(self, shift):
        return lax.rem(self.at + (shift + SIDE), SIDE)

    def copy(self, kind, shift, way):
        block = self.place(shift)
        ref = self.whole(block) if kind < 2 else self.refs(block, kind - 2)
        return pltpu.make_async_remote_copy(
            src_ref=ref,
            dst_ref=ref,
            send_sem=self.send_sem.at[kind],
            recv_sem=self.recv_sem.at[kind],
            device_id=self.device(self.place(way)),
            device_id_type=pl.DeviceIdType.MESH,
        )

    def send(self, kind, shift):
        one = self.copy(kind, shift, 1 if kind % 2 == 0 else -1)
        one.start()
        self.sent.append(one)

    def begin(self):
        self.send(0, 0)
        self.send(1, 0)

    def full(self, kind):
        shift = (-1, 1)[kind]
        self.copy(kind, shift, 1).wait_recv()
        self.send(kind + 2, shift)

    def halves(self):
        self.copy(2, 2, 1).wait_recv()
        self.copy(3, 2, 1).wait_recv()

    def finish(self):
        for one in self.sent:
            one.wait_send()


def project(acc, hid_v, buf, block, first=False):
    part = jnp.dot(hid_v[block], buf[block], preferred_element_type=F32)
    acc[...] = part if first else acc[...] + part


def run_gather(gather, acc, hid_v, buf, first_work, late_work, last_work):
    def work(*pairs):
        for dx, dy in pairs:
            project(acc, hid_v, buf, gather.block(dx, dy))

    first_work()
    gather.fulls(1, 0)
    gather.fulls(2, 0)
    work((-1, 0), (1, 0), (0, -1), (0, 1))
    gather.quarters(1, 0)
    gather.fulls(2, 1)
    gather.fulls(2, 2)
    work((-1, -1), (1, -1), (-1, 1), (1, 1))
    gather.quarters(2, 0)
    work((2, 0), (0, 2))
    late_work()
    gather.fulls(2, 3)
    gather.quarters(2, 1)
    gather.quarters(2, 2)
    work((2, -1), (2, 1), (-1, 2), (1, 2))
    gather.quarters(2, 3)
    last_work()
    work((2, 2))


def body(
    hid, wq, wk, wv, ck, cv, ks_h, vs_h, sel_h, cnt_h,
    att_o, bk_o, bv_o,
    hid_v, wkv_buf, wq_buf, acc_kv, acc_q, pkv_in, pq_in, cache_v, kv,
    ks, vs, sel, cnt, q_stage, qbuf, peak, mass, accum,
    r_out, r_in, s_out, s_in, fin, att_in,
    local_sem, out_sem, hid_sem, part_sem, sib_send, sib_recv,
    akv_send, akv_recv, aq_send, aq_recv, ring_kv_send, ring_kv_recv, ring_q_send, ring_q_recv,
    sel_send, sel_recv, qy_send, qy_recv, r_send, r_recv, s_send, s_recv, f_send, f_recv,
):
    chip, core = position()
    at_x, at_y = lax.rem(chip, SIDE), lax.div(chip, SIDE)
    sibling = device_of(chip, 1 - core)

    def in_row(x):
        return device_of(at_y * SIDE + x, core)

    def in_column(y):
        return device_of(y * SIDE + at_x, core)

    def remote(src, dst, send_sem, recv_sem, device):
        return pltpu.make_async_remote_copy(
            src_ref=src, dst_ref=dst, send_sem=send_sem, recv_sem=recv_sem,
            device_id=device, device_id_type=pl.DeviceIdType.MESH,
        )

    barrier = pltpu.get_barrier_semaphore()

    def greet(device):
        pl.semaphore_signal(barrier, inc=1, device_id=device, device_id_type=pl.DeviceIdType.MESH)

    greet(sibling)
    for step in (1, 2, 3):
        greet(in_row(lax.rem(at_x + step, SIDE)))
        greet(in_column(lax.rem(at_y + step, SIDE)))

    loads = [
        pltpu.make_async_copy(wk, wkv_buf.at[chip, :, pl.ds(0, HEAD_DIM)], local_sem.at[0]),
        pltpu.make_async_copy(wv, wkv_buf.at[chip, :, pl.ds(HEAD_DIM, HEAD_DIM)], local_sem.at[1]),
        pltpu.make_async_copy(wq, wq_buf.at[chip], local_sem.at[2]),
        pltpu.make_async_copy(ck.at[0], cache_v.at[0], local_sem.at[3]),
        pltpu.make_async_copy(cv.at[0], cache_v.at[1], local_sem.at[4]),
        pltpu.make_async_copy(ks_h, ks, local_sem.at[6]),
        pltpu.make_async_copy(vs_h, vs, local_sem.at[7]),
        pltpu.make_async_copy(sel_h, sel.at[at_y], local_sem.at[8]),
        pltpu.make_async_copy(cnt_h, cnt, local_sem.at[9]),
    ]
    for one in loads:
        one.start()

    def load_hidden(block, carry):
        start = pl.multiple_of((block * 2 + core) * DEPTH, DEPTH)
        pltpu.make_async_copy(
            hid.at[0, :, pl.ds(start, DEPTH)], hid_v.at[block, pl.ds(0, SLOTS), :], local_sem.at[5]
        ).start()
        return carry

    lax.fori_loop(0, CHIPS, load_hidden, 0)
    pl.semaphore_wait(barrier, 7)

    gkv = Gather(wkv_buf, DEPTH // 2, DEPTH, chip, core, akv_send, akv_recv)
    gq = Gather(wq_buf, DEPTH // 4, DEPTH, chip, core, aq_send, aq_recv)
    loads[0].wait()
    loads[1].wait()
    gkv.begin()
    loads[2].wait()
    gq.begin()

    def send_hidden(block, carry):
        start = pl.multiple_of((block * 2 + 1 - core) * DEPTH, DEPTH)
        remote(
            hid.at[0, :, pl.ds(start, DEPTH)], hid_v.at[block, pl.ds(SLOTS, SLOTS), :],
            hid_sem.at[0], hid_sem.at[1], sibling,
        ).start()
        return carry

    lax.fori_loop(0, CHIPS, send_hidden, 0)
    hid_own = hid_v.at[:, pl.ds(0, SLOTS), :]
    hid_far = hid_v.at[:, pl.ds(SLOTS, SLOTS), :]
    hid_copy = remote(hid_far, hid_far, hid_sem.at[0], hid_sem.at[1], sibling)

    for one in loads[3:]:
        one.wait()

    def column_copy(src, dst, sends, recvs, step, back):
        slot = step - 1
        other = lax.rem(at_y + (SIDE - step if back else step), SIDE)
        return remote(src(other), dst(other if back else at_y), sends.at[slot], recvs.at[slot], in_column(other))

    def sel_copy(step, back):
        return column_copy(
            lambda other: sel.at[other if back else at_y], lambda row: sel.at[row],
            sel_send, sel_recv, step, back,
        )

    for step in (1, 2, 3):
        sel_copy(step, False).start()

    for which, scale in enumerate((ks, vs)):
        for part in range(SPAN_LEN // 128):
            rows = slice(part * 128, (part + 1) * 128)
            spread = jnp.transpose(jnp.broadcast_to(scale[0, :, rows], (128, 128)))
            kv[at_y, which, core, rows, :] = (cache_v[which, rows, :].astype(F32) * spread).astype(BF16)

    def first_kv():
        pltpu.make_async_copy(hid_own, hid_own, local_sem.at[5]).wait()
        hid_copy.wait_recv()
        project(acc_kv, hid_v, wkv_buf, chip, first=True)
        project(acc_q, hid_v, wq_buf, chip, first=True)

    run_gather(gkv, acc_kv, hid_v, wkv_buf, first_kv, lambda: None, lambda: None)
    kv_part = remote(
        acc_kv.at[pl.ds(SLOTS, SLOTS), :], pkv_in, part_sem.at[0], part_sem.at[1], sibling
    )
    kv_part.start()
    count = cnt[0]
    slot_row = lax.broadcasted_iota(jnp.int32, (1, SLOTS), 1)
    wanted = jnp.where(slot_row < count, sel[at_y], -1)

    ring_kv = Ring(
        lambda row, which: kv.at[row, which, core], lambda row: kv.at[row, :, core],
        at_y, in_column, ring_kv_send, ring_kv_recv,
    )
    ring_q = Ring(
        lambda x, which: qbuf.at[x, pl.ds(which * 2, 2)], lambda x: qbuf.at[x],
        at_x, in_row, ring_q_send, ring_q_recv,
    )

    def to_sibling(shift, owner):
        block = ring_kv.place(shift)
        ref = kv.at[block, :, owner]
        return remote(ref, ref, sib_send.at[shift + 1], sib_recv.at[shift + 1], sibling)

    k_out = pltpu.make_async_copy(kv.at[at_y, 0, core], bk_o.at[0], out_sem.at[0])
    v_out = pltpu.make_async_copy(kv.at[at_y, 1, core], bv_o.at[0], out_sem.at[1])

    def blend():
        kv_part.wait_recv()
        fresh = (acc_kv[0:SLOTS, :] + pkv_in[...]).astype(BF16)
        ones = jnp.ones((SLOTS, HEAD_DIM), BF16)

        def part(step, carry):
            start = pl.multiple_of(step * 128, 128)
            rows = lax.broadcasted_iota(jnp.int32, (128, SLOTS), 0) + start
            chosen = jnp.where(rows == wanted, 1.0, 0.0).astype(BF16)
            moved = jnp.dot(chosen, fresh, preferred_element_type=F32)
            hit = jnp.dot(chosen, ones, preferred_element_type=F32) > 0.5
            for which in (0, 1):
                new = moved[:, which * HEAD_DIM:(which + 1) * HEAD_DIM]
                old = kv[at_y, which, core, pl.ds(start, 128), :].astype(F32)
                kv[at_y, which, core, pl.ds(start, 128), :] = jnp.where(hit, new, old).astype(BF16)
            return carry

        lax.fori_loop(0, SPAN_LEN // 128, part, 0)
        ring_kv.begin()
        to_sibling(0, core).start()
        k_out.start()
        v_out.start()

    def pass_kv():
        for kind, shift in ((0, -1), (1, 1)):
            ring_kv.full(kind)
            to_sibling(shift, core).start()

    def end_kv():
        ring_kv.halves()
        to_sibling(2, core).start()

    run_gather(gq, acc_q, hid_v, wq_buf, blend, pass_kv, end_kv)
    q_part = remote(acc_q.at[pl.ds(SLOTS, SLOTS), :], pq_in, part_sem.at[2], part_sem.at[3], sibling)
    q_part.start()
    peak[...] = jnp.full((SIDE, ROWS, 128), -1e30, F32)
    mass[...] = jnp.zeros((SIDE, ROWS, 128), F32)
    accum[...] = jnp.zeros((SIDE, ROWS, HEAD_DIM), F32)
    q_part.wait_recv()
    for g in range(GROUP):
        cols = slice(g * HEAD_DIM, (g + 1) * HEAD_DIM)
        q_stage[g] = (acc_q[0:SLOTS, cols] + pq_in[:, cols]).astype(BF16)

    def qy_copy(step, back):
        return column_copy(
            lambda other: q_stage.at[other], lambda row: qbuf.at[at_x, row], qy_send, qy_recv, step, back
        )

    for step in (1, 2, 3):
        qy_copy(step, False).start()
    qbuf[at_x, at_y] = q_stage[at_y]
    for shift in (0, -1, 1, 2):
        to_sibling(shift, 1 - core).wait_recv()
    for step in (1, 2, 3):
        qy_copy(step, True).wait_recv()
        sel_copy(step, True).wait_recv()
    ring_q.begin()

    def scored(x, row, block):
        keys = kv[block, 0].reshape(KEYS, HEAD_DIM)
        return lax.dot_general(
            qbuf[x, row], keys, (((1,), (1,)), ((), ())), preferred_element_type=F32
        )

    def attend(x, pairs, masked):
        ahead = scored(x, *pairs[0])
        for index, (row, block) in enumerate(pairs):
            here = slice(row * SLOTS, (row + 1) * SLOTS)
            scores = ahead
            if index + 1 < len(pairs):
                ahead = scored(x, *pairs[index + 1])
            if masked:
                key = lax.broadcasted_iota(jnp.int32, (SLOTS, KEYS), 1)
                place = jnp.transpose(jnp.broadcast_to(sel[row], (128, 128)))[:, 0:1] + core * SPAN_LEN
                scores = jnp.where(key <= place, scores, -1e30)
            before = peak[x, here, :]
            best = jnp.maximum(before, jnp.max(scores, axis=1, keepdims=True))
            fade = jnp.exp2((before - best) * EXP2_SCALE)
            weights = jnp.exp2((scores - best[:, 0:1]) * EXP2_SCALE)
            peak[x, here, :] = best
            mass[x, here, :] = mass[x, here, :] * fade + jnp.sum(weights, axis=1, keepdims=True)
            accum[x, here, :] = accum[x, here, :] * fade + jnp.dot(
                weights.astype(BF16), kv[block, 1].reshape(KEYS, HEAD_DIM), preferred_element_type=F32
            )

    earlier = [(1, 0), (2, 0), (3, 0), (2, 1), (3, 1), (3, 2)]
    level = [(0, 0), (1, 1), (2, 2), (3, 3)]

    def r_copy(step, back):
        slot = step - 1
        other = lax.rem(at_x + (SIDE - step if back else step), SIDE)
        return (
            remote(
                r_out.at[other], r_in.at[other if back else at_x],
                r_send.at[slot], r_recv.at[slot], in_row(other),
            ),
            remote(
                s_out.at[other], s_in.at[other if back else at_x],
                s_send.at[slot], s_recv.at[slot], in_row(other),
            ),
        )

    def stats(x):
        lane = lax.broadcasted_iota(jnp.int32, (ROWS, 128), 1)
        both = jnp.where(lane == 0, peak[x], mass[x])
        return jnp.transpose(both)[0:8, :]

    def one_chip(index, carry):
        step = jnp.where(index == 0, 0, jnp.where(index == 1, 3, jnp.where(index == 2, 1, 2)))
        x = lax.rem(at_x + step, SIDE)

        @pl.when(index == 1)
        def _():
            ring_q.full(0)

        @pl.when(index == 2)
        def _():
            ring_q.full(1)

        @pl.when(index == 3)
        def _():
            ring_q.halves()

        attend(x, earlier, False)

        @pl.when(x > at_x)
        def _():
            attend(x, level, False)

        @pl.when(index > 0)
        def _():
            r_out[x] = accum[x].astype(BF16)
            s_out[x] = stats(x)

        for which, way in ((1, 3), (2, 1), (3, 2)):
            @pl.when(index == which)
            def _(way=way):
                for one in r_copy(way, False):
                    one.start()

        return carry

    lax.fori_loop(0, SIDE, one_chip, 0)
    attend(at_x, level, True)
    s_in[at_x] = stats(at_x)
    for step in (1, 3, 2):
        for one in r_copy(step, True):
            one.wait_recv()
    seen = s_in[...]
    bests = seen[:, 0:1, :]
    top = jnp.max(bests, axis=0, keepdims=True)
    factor = jnp.exp2((bests - top) * EXP2_SCALE)
    total = jnp.sum(factor * seen[:, 1:2, :], axis=0, keepdims=True)
    factor = jnp.broadcast_to(factor / total, (SIDE, 32, ROWS)).reshape(SIDE * 32, ROWS)
    factor = jnp.transpose(factor)
    r_in[at_x] = accum[at_x].astype(BF16)
    merged = jnp.zeros((ROWS, HEAD_DIM), F32)
    for x in range(SIDE):
        merged += r_in[x].astype(F32) * factor[:, x * 32:x * 32 + 1]
    fin[...] = merged.reshape(SIDE, SLOTS, HEAD_DIM).astype(BF16)

    def f_copy(step, back):
        return column_copy(
            lambda other: fin.at[other], lambda row: att_in.at[row], f_send, f_recv, step, back
        )

    for step in (1, 2, 3):
        f_copy(step, False).start()
    att_in[at_y] = fin[at_y]
    for step in (1, 2, 3):
        f_copy(step, True).wait_recv()
    used = lax.broadcasted_iota(jnp.int32, (SLOTS, HEAD_DIM), 0) < count
    for g in range(GROUP):
        cols = slice(g * HEAD_DIM, (g + 1) * HEAD_DIM)
        att_o[0, :, cols] = jnp.where(used, att_in[g].astype(F32), 0.0).astype(BF16)

    gkv.finish()
    gq.finish()
    ring_kv.finish()
    for kind in range(4):
        ring_q.copy(kind, 0, 1).wait_send()
    hid_copy.wait_send()
    kv_part.wait_send()
    q_part.wait_send()
    for shift in (0, -1, 1, 2):
        to_sibling(shift, core).wait_send()
    for step in (1, 2, 3):
        sel_copy(step, False).wait_send()
        qy_copy(step, False).wait_send()
        f_copy(step, False).wait_send()
        for one in r_copy(step, False):
            one.wait_send()
    for one in (k_out, v_out):
        one.wait()


def shards(hidden_rows, w_query, w_key, w_value, cache_keys, cache_values, key_scale, value_scale, sel_index, sel_count):
    hbm_spec = pl.BlockSpec(memory_space=pltpu.HBM)
    dma = pltpu.SemaphoreType.DMA
    return pl.pallas_call(
        body,
        out_shape=(
            pltpu.VMEM((1, SLOTS, ROWS), BF16),
            pltpu.VMEM((1, SPAN_LEN, HEAD_DIM), BF16),
            pltpu.VMEM((1, SPAN_LEN, HEAD_DIM), BF16),
        ),
        in_specs=[hbm_spec] * 10,
        out_specs=(pl.BlockSpec(memory_space=pltpu.VMEM),) * 3,
        scratch_shapes=[
            pltpu.VMEM((CHIPS, 2 * SLOTS, DEPTH), BF16),
            pltpu.VMEM((CHIPS, DEPTH, 2 * HEAD_DIM), BF16),
            pltpu.VMEM((CHIPS, DEPTH, ROWS), BF16),
            pltpu.VMEM((2 * SLOTS, 2 * HEAD_DIM), F32),
            pltpu.VMEM((2 * SLOTS, ROWS), F32),
            pltpu.VMEM((SLOTS, 2 * HEAD_DIM), F32),
            pltpu.VMEM((SLOTS, ROWS), F32),
            pltpu.VMEM((2, SPAN_LEN, HEAD_DIM), BF16),
            pltpu.VMEM((SIDE, 2, 2, SPAN_LEN, HEAD_DIM), BF16),
            pltpu.VMEM((1, 1, SPAN_LEN), F32),
            pltpu.VMEM((1, 1, SPAN_LEN), F32),
            pltpu.VMEM((SIDE, 1, SLOTS), jnp.int32),
            pltpu.SMEM((1,), jnp.int32),
            pltpu.VMEM((GROUP, SLOTS, HEAD_DIM), BF16),
            pltpu.VMEM((SIDE, SIDE, SLOTS, HEAD_DIM), BF16),
            pltpu.VMEM((SIDE, ROWS, 128), F32),
            pltpu.VMEM((SIDE, ROWS, 128), F32),
            pltpu.VMEM((SIDE, ROWS, HEAD_DIM), F32),
            pltpu.VMEM((SIDE, ROWS, HEAD_DIM), BF16),
            pltpu.VMEM((SIDE, ROWS, HEAD_DIM), BF16),
            pltpu.VMEM((SIDE, 8, ROWS), F32),
            pltpu.VMEM((SIDE, 8, ROWS), F32),
            pltpu.VMEM((SIDE, SLOTS, HEAD_DIM), BF16),
            pltpu.VMEM((SIDE, SLOTS, HEAD_DIM), BF16),
            dma((10,)), dma((2,)), dma((2,)), dma((4,)), dma((4,)), dma((4,)),
            dma((40,)), dma((40,)), dma((40,)), dma((40,)), dma((4,)), dma((4,)), dma((4,)), dma((4,)),
            dma((3,)), dma((3,)), dma((3,)), dma((3,)), dma((3,)), dma((3,)), dma((3,)), dma((3,)), dma((3,)), dma((3,)),
        ],
        compiler_params=pltpu.CompilerParams(
            collective_id=0, has_side_effects=True, vmem_limit_bytes=63 * 1024 * 1024
        ),
        name="span_attention",
    )(hidden_rows, w_query, w_key, w_value, cache_keys, cache_values, key_scale, value_scale, sel_index, sel_count)


def solution(mesh):
    placed = (
        P(("req", "span"), None, None),
        P("span", "head"),
        P("span", "head"),
        P("span", "head"),
        P(("req", "span"), None, "head"),
        P(("req", "span"), None, "head"),
        P(("req", "span"), "head", None),
        P(("req", "span"), "head", None),
        P(("req", "span"), None),
        P(("req", "span")),
    )
    return jax.shard_map(
        shards,
        mesh=mesh,
        in_specs=placed,
        out_specs=(
            P(("req", "span"), None, "head"),
            P(("req", "span"), None, "head"),
            P(("req", "span"), None, "head"),
        ),
        check_vma=False,
    )
```

```python
import functools
import math

import jax
import jax.numpy as jnp
from jax import lax
from jax.experimental import pallas as pl
from jax.experimental.pallas import tpu as pltpu
from jax.sharding import PartitionSpec as P

HEAD_DIM = 128
GROUP = 4
SLOTS = 128
SPAN_LEN = 1024
SIDE = 4
CHIPS = SIDE * SIDE
DEPTH = 256
ROWS = GROUP * SLOTS
KEYS = 2 * SPAN_LEN
EXP2_SCALE = math.log2(math.e) / math.sqrt(HEAD_DIM)
F32 = jnp.float32
BF16 = jnp.bfloat16
OFFSETS = (0, -1, 1, 2)


def position():
    span = lax.axis_index("span")
    core = lax.rem(span, 2)
    chip = lax.div(span, 2)
    return chip, core


def device_of(chip, core):
    return {"span": chip * 2 + core}


class Gather:
    def __init__(self, buf, first, rows, chip, core, send_sem, recv_sem):
        self.buf, self.first, self.rows, self.chip, self.core = buf, first, rows, chip, core
        self.send_sem, self.recv_sem = send_sem, recv_sem
        self.at = (lax.rem(chip, SIDE), lax.div(chip, SIDE))
        self.sent = []

    def block(self, dx, dy):
        x = lax.rem(self.at[0] + (dx + SIDE), SIDE)
        y = lax.rem(self.at[1] + (dy + SIDE), SIDE)
        return y * SIDE + x

    def along(self, axis, first, second):
        return self.block(first, second) if axis == 0 else self.block(second, first)

    def piece(self, half, block, kind):
        size = self.first if half == 0 else self.rows - self.first
        start = half * self.first
        if kind >= 2:
            size //= 2
            start += (kind - 2) * size
        return self.buf.at[block, pl.ds(start, size), :]

    def copy(self, half, stage, j, kind, block, target):
        where = half * 20 + (kind if stage == 1 else 4 + j * 4 + kind)
        ref = self.piece(half, block, kind)
        return pltpu.make_async_remote_copy(
            src_ref=ref,
            dst_ref=ref,
            send_sem=self.send_sem.at[where],
            recv_sem=self.recv_sem.at[where],
            device_id=device_of(target, self.core),
            device_id_type=pl.DeviceIdType.MESH,
        )

    def locate(self, half, stage, j, shift):
        if stage == 1:
            return self.along(half, shift, 0)
        return self.along(half, OFFSETS[j], shift)

    def step(self, half, stage, way):
        axis = half if stage == 1 else 1 - half
        return self.along(axis, way, 0)

    def send(self, half, stage, j, kind, shift):
        way = 1 if kind % 2 == 0 else -1
        one = self.copy(half, stage, j, kind, self.locate(half, stage, j, shift), self.step(half, stage, way))
        one.start()
        self.sent.append(one)

    def receive(self, half, stage, j, kind):
        shift = (-1, 1, 2, 2)[kind]
        self.copy(half, stage, j, kind, self.locate(half, stage, j, shift), self.chip).wait_recv()

    def spread(self, half, stage, j):
        self.send(half, stage, j, 0, 0)
        self.send(half, stage, j, 1, 0)

    def begin(self):
        for half in (0, 1):
            self.spread(half, 1, 0)
        for half in (0, 1):
            self.spread(half, 2, 0)

    def fulls(self, stage, j):
        for kind in (0, 1):
            for half in (0, 1):
                self.receive(half, stage, j, kind)
                self.send(half, stage, j, kind + 2, (-1, 1)[kind])
                if stage == 1:
                    self.spread(half, 2, 1 + kind)

    def quarters(self, stage, j):
        for half in (0, 1):
            for kind in (2, 3):
                self.receive(half, stage, j, kind)
            if stage == 1:
                self.spread(half, 2, 3)

    def finish(self):
        for one in self.sent:
            one.wait_send()


class Ring:
    def __init__(self, refs, whole, at, device, send_sem, recv_sem):
        self.refs, self.whole, self.at, self.device = refs, whole, at, device
        self.send_sem, self.recv_sem = send_sem, recv_sem
        self.sent = []

    def place(self, shift):
        return lax.rem(self.at + (shift + SIDE), SIDE)

    def copy(self, kind, shift, way):
        block = self.place(shift)
        ref = self.whole(block) if kind < 2 else self.refs(block, kind - 2)
        return pltpu.make_async_remote_copy(
            src_ref=ref,
            dst_ref=ref,
            send_sem=self.send_sem.at[kind],
            recv_sem=self.recv_sem.at[kind],
            device_id=self.device(self.place(way)),
            device_id_type=pl.DeviceIdType.MESH,
        )

    def send(self, kind, shift):
        one = self.copy(kind, shift, 1 if kind % 2 == 0 else -1)
        one.start()
        self.sent.append(one)

    def begin(self):
        self.send(0, 0)
        self.send(1, 0)

    def full(self, kind):
        shift = (-1, 1)[kind]
        self.copy(kind, shift, 1).wait_recv()
        self.send(kind + 2, shift)

    def halves(self):
        self.copy(2, 2, 1).wait_recv()
        self.copy(3, 2, 1).wait_recv()

    def finish(self):
        for one in self.sent:
            one.wait_send()


def project(acc, hid_v, buf, block, first=False):
    part = jnp.dot(hid_v[block], buf[block], preferred_element_type=F32)
    acc[...] = part if first else acc[...] + part


def run_gather(gather, acc, hid_v, buf, **hooks):
    def hook(name):
        if name in hooks:
            hooks[name]()

    def work(*pairs):
        for dx, dy in pairs:
            project(acc, hid_v, buf, gather.block(dx, dy))

    hook("start")
    gather.fulls(1, 0)
    hook("one")
    gather.fulls(2, 0)
    hook("two")
    work((-1, 0), (1, 0), (0, -1), (0, 1))
    gather.quarters(1, 0)
    gather.fulls(2, 1)
    hook("three")
    gather.fulls(2, 2)
    hook("four")
    work((-1, -1), (1, -1), (-1, 1), (1, 1))
    gather.quarters(2, 0)
    work((2, 0), (0, 2))
    hook("five")
    gather.fulls(2, 3)
    gather.quarters(2, 1)
    gather.quarters(2, 2)
    work((2, -1), (2, 1), (-1, 2), (1, 2))
    gather.quarters(2, 3)
    hook("six")
    work((2, 2))


def body(
    hid, wq, wk, wv, ck, cv, ks_h, vs_h, sel_h, cnt_h,
    att_o, bk_o, bv_o,
    hid_v, wkv_buf, wq_buf, acc_kv, acc_q, pkv_in, pq_in, cache_v, kv,
    ks, vs, sel, cnt, q_stage, qbuf, peak, mass, accum,
    r_out, r_in, s_out, s_in, fin, att_in,
    local_sem, out_sem, hid_sem, part_sem, sib_send, sib_recv,
    akv_send, akv_recv, aq_send, aq_recv, ring_kv_send, ring_kv_recv, ring_q_send, ring_q_recv,
    sel_send, sel_recv, qy_send, qy_recv, r_send, r_recv, s_send, s_recv, f_send, f_recv,
):
    chip, core = position()
    at_x, at_y = lax.rem(chip, SIDE), lax.div(chip, SIDE)
    sibling = device_of(chip, 1 - core)

    def in_row(x):
        return device_of(at_y * SIDE + x, core)

    def in_column(y):
        return device_of(y * SIDE + at_x, core)

    def remote(src, dst, send_sem, recv_sem, device):
        return pltpu.make_async_remote_copy(
            src_ref=src, dst_ref=dst, send_sem=send_sem, recv_sem=recv_sem,
            device_id=device, device_id_type=pl.DeviceIdType.MESH,
        )

    barrier = pltpu.get_barrier_semaphore()

    def greet(device):
        pl.semaphore_signal(barrier, inc=1, device_id=device, device_id_type=pl.DeviceIdType.MESH)

    greet(sibling)
    for step in (1, 2, 3):
        greet(in_row(lax.rem(at_x + step, SIDE)))
        greet(in_column(lax.rem(at_y + step, SIDE)))

    loads = [
        pltpu.make_async_copy(wk, wkv_buf.at[chip, :, pl.ds(0, HEAD_DIM)], local_sem.at[0]),
        pltpu.make_async_copy(wv, wkv_buf.at[chip, :, pl.ds(HEAD_DIM, HEAD_DIM)], local_sem.at[1]),
        pltpu.make_async_copy(wq, wq_buf.at[chip], local_sem.at[2]),
        pltpu.make_async_copy(ck.at[0], cache_v.at[0], local_sem.at[3]),
        pltpu.make_async_copy(cv.at[0], cache_v.at[1], local_sem.at[4]),
        pltpu.make_async_copy(ks_h, ks, local_sem.at[6]),
        pltpu.make_async_copy(vs_h, vs, local_sem.at[7]),
        pltpu.make_async_copy(sel_h, sel.at[at_y], local_sem.at[8]),
        pltpu.make_async_copy(cnt_h, cnt, local_sem.at[9]),
    ]
    for one in loads:
        one.start()

    def load_hidden(block, carry):
        start = pl.multiple_of((block * 2 + core) * DEPTH, DEPTH)
        pltpu.make_async_copy(
            hid.at[0, :, pl.ds(start, DEPTH)], hid_v.at[block, pl.ds(0, SLOTS), :], local_sem.at[5]
        ).start()
        return carry

    lax.fori_loop(0, CHIPS, load_hidden, 0)
    pl.semaphore_wait(barrier, 7)

    gkv = Gather(wkv_buf, DEPTH // 2, DEPTH, chip, core, akv_send, akv_recv)
    gq = Gather(wq_buf, DEPTH // 4, DEPTH, chip, core, aq_send, aq_recv)
    loads[0].wait()
    loads[1].wait()
    gkv.begin()
    loads[2].wait()

    def send_hidden(block, carry):
        start = pl.multiple_of((block * 2 + 1 - core) * DEPTH, DEPTH)
        remote(
            hid.at[0, :, pl.ds(start, DEPTH)], hid_v.at[block, pl.ds(SLOTS, SLOTS), :],
            hid_sem.at[0], hid_sem.at[1], sibling,
        ).start()
        return carry

    lax.fori_loop(0, CHIPS, send_hidden, 0)
    hid_own = hid_v.at[:, pl.ds(0, SLOTS), :]
    hid_far = hid_v.at[:, pl.ds(SLOTS, SLOTS), :]
    hid_copy = remote(hid_far, hid_far, hid_sem.at[0], hid_sem.at[1], sibling)

    for one in loads[3:]:
        one.wait()

    def column_copy(src, dst, sends, recvs, step, back):
        slot = step - 1
        other = lax.rem(at_y + (SIDE - step if back else step), SIDE)
        return remote(src(other), dst(other if back else at_y), sends.at[slot], recvs.at[slot], in_column(other))

    def sel_copy(step, back):
        return column_copy(
            lambda other: sel.at[other if back else at_y], lambda row: sel.at[row],
            sel_send, sel_recv, step, back,
        )

    for step in (1, 2, 3):
        sel_copy(step, False).start()

    for which, scale in enumerate((ks, vs)):
        for part in range(SPAN_LEN // 128):
            rows = slice(part * 128, (part + 1) * 128)
            spread = jnp.transpose(jnp.broadcast_to(scale[0, :, rows], (128, 128)))
            kv[at_y, which, core, rows, :] = (cache_v[which, rows, :].astype(F32) * spread).astype(BF16)

    def first_kv():
        pltpu.make_async_copy(hid_own, hid_own, local_sem.at[5]).wait()
        hid_copy.wait_recv()
        project(acc_kv, hid_v, wkv_buf, chip, first=True)
        project(acc_q, hid_v, wq_buf, chip, first=True)

    run_gather(gkv, acc_kv, hid_v, wkv_buf, start=first_kv, six=gq.begin)
    kv_part = remote(
        acc_kv.at[pl.ds(SLOTS, SLOTS), :], pkv_in, part_sem.at[0], part_sem.at[1], sibling
    )
    kv_part.start()
    count = cnt[0]
    slot_row = lax.broadcasted_iota(jnp.int32, (1, SLOTS), 1)
    wanted = jnp.where(slot_row < count, sel[at_y], -1)

    rings = [
        Ring(
            lambda row, half, which=which: kv.at[row, which, core, pl.ds(half * 512, 512)],
            lambda row, which=which: kv.at[row, which, core],
            at_y, in_column, ring_kv_send.at[which], ring_kv_recv.at[which],
        )
        for which in (0, 1)
    ]
    ring_q = Ring(
        lambda x, which: qbuf.at[x, pl.ds(which * 2, 2)], lambda x: qbuf.at[x],
        at_x, in_row, ring_q_send, ring_q_recv,
    )

    def to_sibling(which, shift, owner):
        ref = kv.at[rings[which].place(shift), which, owner]
        return remote(ref, ref, sib_send.at[which, shift + 1], sib_recv.at[which, shift + 1], sibling)

    k_out = pltpu.make_async_copy(kv.at[at_y, 0, core], bk_o.at[0], out_sem.at[0])
    v_out = pltpu.make_async_copy(kv.at[at_y, 1, core], bv_o.at[0], out_sem.at[1])

    def blend():
        kv_part.wait_recv()
        fresh = (acc_kv[0:SLOTS, :] + pkv_in[...]).astype(BF16)
        ones = jnp.ones((SLOTS, HEAD_DIM), BF16)

        for step in range(SPAN_LEN // 128):
            here = slice(step * 128, (step + 1) * 128)
            rows = lax.broadcasted_iota(jnp.int32, (128, SLOTS), 0) + step * 128
            chosen = jnp.where(rows == wanted, 1.0, 0.0).astype(BF16)
            moved = jnp.dot(chosen, fresh, preferred_element_type=F32)
            hit = jnp.dot(chosen, ones, preferred_element_type=F32) > 0.5
            for which in (0, 1):
                new = moved[:, which * HEAD_DIM:(which + 1) * HEAD_DIM]
                old = kv[at_y, which, core, here, :].astype(F32)
                kv[at_y, which, core, here, :] = jnp.where(hit, new, old).astype(BF16)

        for which in (0, 1):
            rings[which].begin()
        for which in (0, 1):
            to_sibling(which, 0, core).start()
        k_out.start()
        v_out.start()

    def pass_on(which):
        for kind, shift in ((0, -1), (1, 1)):
            rings[which].full(kind)
            to_sibling(which, shift, core).start()

    def end(which):
        rings[which].halves()
        to_sibling(which, 2, core).start()

    pass_k, pass_v = functools.partial(pass_on, 0), functools.partial(pass_on, 1)
    end_k, end_v = functools.partial(end, 0), functools.partial(end, 1)
    run_gather(gq, acc_q, hid_v, wq_buf, start=blend, two=pass_k, three=pass_v, five=end_k, six=end_v)
    q_part = remote(acc_q.at[pl.ds(SLOTS, SLOTS), :], pq_in, part_sem.at[2], part_sem.at[3], sibling)
    q_part.start()
    peak[...] = jnp.full((SIDE, ROWS, 128), -1e30, F32)
    mass[...] = jnp.zeros((SIDE, ROWS, 128), F32)
    accum[...] = jnp.zeros((SIDE, ROWS, HEAD_DIM), F32)
    q_part.wait_recv()
    for g in range(GROUP):
        cols = slice(g * HEAD_DIM, (g + 1) * HEAD_DIM)
        q_stage[g] = (acc_q[0:SLOTS, cols] + pq_in[:, cols]).astype(BF16)

    def qy_copy(step, back):
        return column_copy(
            lambda other: q_stage.at[other], lambda row: qbuf.at[at_x, row], qy_send, qy_recv, step, back
        )

    for step in (1, 2, 3):
        qy_copy(step, False).start()
    qbuf[at_x, at_y] = q_stage[at_y]
    for shift in (0, -1, 1, 2):
        for which in (0, 1):
            to_sibling(which, shift, 1 - core).wait_recv()
    for step in (1, 2, 3):
        qy_copy(step, True).wait_recv()
        sel_copy(step, True).wait_recv()
    ring_q.begin()

    def scored(x, row, block):
        keys = kv[block, 0].reshape(KEYS, HEAD_DIM)
        return lax.dot_general(
            qbuf[x, row], keys, (((1,), (1,)), ((), ())), preferred_element_type=F32
        )

    def attend(x, pairs, masked):
        ahead = scored(x, *pairs[0])
        for index, (row, block) in enumerate(pairs):
            here = slice(row * SLOTS, (row + 1) * SLOTS)
            scores = ahead
            if index + 1 < len(pairs):
                ahead = scored(x, *pairs[index + 1])
            if masked:
                key = lax.broadcasted_iota(jnp.int32, (SLOTS, KEYS), 1)
                place = jnp.transpose(jnp.broadcast_to(sel[row], (128, 128)))[:, 0:1] + core * SPAN_LEN
                scores = jnp.where(key <= place, scores, -1e30)
            before = peak[x, here, :]
            best = jnp.maximum(before, jnp.max(scores, axis=1, keepdims=True))
            fade = jnp.exp2((before - best) * EXP2_SCALE)
            weights = jnp.exp2((scores - best[:, 0:1]) * EXP2_SCALE)
            peak[x, here, :] = best
            mass[x, here, :] = mass[x, here, :] * fade + jnp.sum(weights, axis=1, keepdims=True)
            accum[x, here, :] = accum[x, here, :] * fade + jnp.dot(
                weights.astype(BF16), kv[block, 1].reshape(KEYS, HEAD_DIM), preferred_element_type=F32
            )

    earlier = [(1, 0), (2, 0), (3, 0), (2, 1), (3, 1), (3, 2)]
    level = [(0, 0), (1, 1), (2, 2), (3, 3)]

    def r_copy(step, back):
        slot = step - 1
        other = lax.rem(at_x + (SIDE - step if back else step), SIDE)
        return (
            remote(
                r_out.at[other], r_in.at[other if back else at_x],
                r_send.at[slot], r_recv.at[slot], in_row(other),
            ),
            remote(
                s_out.at[other], s_in.at[other if back else at_x],
                s_send.at[slot], s_recv.at[slot], in_row(other),
            ),
        )

    def stats(x):
        lane = lax.broadcasted_iota(jnp.int32, (ROWS, 128), 1)
        both = jnp.where(lane == 0, peak[x], mass[x])
        return jnp.transpose(both)[0:8, :]

    def one_chip(index, carry):
        step = jnp.where(index == 0, 0, jnp.where(index == 1, 3, jnp.where(index == 2, 1, 2)))
        x = lax.rem(at_x + step, SIDE)

        @pl.when(index == 1)
        def _():
            ring_q.full(0)

        @pl.when(index == 2)
        def _():
            ring_q.full(1)

        @pl.when(index == 3)
        def _():
            ring_q.halves()

        attend(x, earlier, False)

        @pl.when(x > at_x)
        def _():
            attend(x, level, False)

        @pl.when(index > 0)
        def _():
            r_out[x] = accum[x].astype(BF16)
            s_out[x] = stats(x)

        for which, way in ((1, 3), (2, 1), (3, 2)):
            @pl.when(index == which)
            def _(way=way):
                for one in r_copy(way, False):
                    one.start()

        return carry

    lax.fori_loop(0, SIDE, one_chip, 0)
    attend(at_x, level, True)
    s_in[at_x] = stats(at_x)
    for step in (1, 3, 2):
        for one in r_copy(step, True):
            one.wait_recv()
    seen = s_in[...]
    bests = seen[:, 0:1, :]
    top = jnp.max(bests, axis=0, keepdims=True)
    factor = jnp.exp2((bests - top) * EXP2_SCALE)
    total = jnp.sum(factor * seen[:, 1:2, :], axis=0, keepdims=True)
    factor = jnp.broadcast_to(factor / total, (SIDE, 32, ROWS)).reshape(SIDE * 32, ROWS)
    factor = jnp.transpose(factor)
    r_in[at_x] = accum[at_x].astype(BF16)
    merged = jnp.zeros((ROWS, HEAD_DIM), F32)
    for x in range(SIDE):
        merged += r_in[x].astype(F32) * factor[:, x * 32:x * 32 + 1]
    fin[...] = merged.reshape(SIDE, SLOTS, HEAD_DIM).astype(BF16)

    def f_copy(step, back):
        return column_copy(
            lambda other: fin.at[other], lambda row: att_in.at[row], f_send, f_recv, step, back
        )

    for step in (1, 2, 3):
        f_copy(step, False).start()
    att_in[at_y] = fin[at_y]
    for step in (1, 2, 3):
        f_copy(step, True).wait_recv()
    used = lax.broadcasted_iota(jnp.int32, (SLOTS, HEAD_DIM), 0) < count
    for g in range(GROUP):
        cols = slice(g * HEAD_DIM, (g + 1) * HEAD_DIM)
        att_o[0, :, cols] = jnp.where(used, att_in[g].astype(F32), 0.0).astype(BF16)

    gkv.finish()
    gq.finish()
    for one in rings:
        one.finish()
    for kind in range(4):
        ring_q.copy(kind, 0, 1).wait_send()
    hid_copy.wait_send()
    kv_part.wait_send()
    q_part.wait_send()
    for shift in (0, -1, 1, 2):
        for which in (0, 1):
            to_sibling(which, shift, core).wait_send()
    for step in (1, 2, 3):
        sel_copy(step, False).wait_send()
        qy_copy(step, False).wait_send()
        f_copy(step, False).wait_send()
        for one in r_copy(step, False):
            one.wait_send()
    for one in (k_out, v_out):
        one.wait()


def shards(hidden_rows, w_query, w_key, w_value, cache_keys, cache_values, key_scale, value_scale, sel_index, sel_count):
    hbm_spec = pl.BlockSpec(memory_space=pltpu.HBM)
    dma = pltpu.SemaphoreType.DMA
    return pl.pallas_call(
        body,
        out_shape=(
            pltpu.VMEM((1, SLOTS, ROWS), BF16),
            pltpu.VMEM((1, SPAN_LEN, HEAD_DIM), BF16),
            pltpu.VMEM((1, SPAN_LEN, HEAD_DIM), BF16),
        ),
        in_specs=[hbm_spec] * 10,
        out_specs=(pl.BlockSpec(memory_space=pltpu.VMEM),) * 3,
        scratch_shapes=[
            pltpu.VMEM((CHIPS, 2 * SLOTS, DEPTH), BF16),
            pltpu.VMEM((CHIPS, DEPTH, 2 * HEAD_DIM), BF16),
            pltpu.VMEM((CHIPS, DEPTH, ROWS), BF16),
            pltpu.VMEM((2 * SLOTS, 2 * HEAD_DIM), F32),
            pltpu.VMEM((2 * SLOTS, ROWS), F32),
            pltpu.VMEM((SLOTS, 2 * HEAD_DIM), F32),
            pltpu.VMEM((SLOTS, ROWS), F32),
            pltpu.VMEM((2, SPAN_LEN, HEAD_DIM), BF16),
            pltpu.VMEM((SIDE, 2, 2, SPAN_LEN, HEAD_DIM), BF16),
            pltpu.VMEM((1, 1, SPAN_LEN), F32),
            pltpu.VMEM((1, 1, SPAN_LEN), F32),
            pltpu.VMEM((SIDE, 1, SLOTS), jnp.int32),
            pltpu.SMEM((1,), jnp.int32),
            pltpu.VMEM((GROUP, SLOTS, HEAD_DIM), BF16),
            pltpu.VMEM((SIDE, SIDE, SLOTS, HEAD_DIM), BF16),
            pltpu.VMEM((SIDE, ROWS, 128), F32),
            pltpu.VMEM((SIDE, ROWS, 128), F32),
            pltpu.VMEM((SIDE, ROWS, HEAD_DIM), F32),
            pltpu.VMEM((SIDE, ROWS, HEAD_DIM), BF16),
            pltpu.VMEM((SIDE, ROWS, HEAD_DIM), BF16),
            pltpu.VMEM((SIDE, 8, ROWS), F32),
            pltpu.VMEM((SIDE, 8, ROWS), F32),
            pltpu.VMEM((SIDE, SLOTS, HEAD_DIM), BF16),
            pltpu.VMEM((SIDE, SLOTS, HEAD_DIM), BF16),
            dma((10,)), dma((2,)), dma((2,)), dma((4,)), dma((2, 4)), dma((2, 4)),
            dma((40,)), dma((40,)), dma((40,)), dma((40,)), dma((2, 4)), dma((2, 4)), dma((4,)), dma((4,)),
            dma((3,)), dma((3,)), dma((3,)), dma((3,)), dma((3,)), dma((3,)), dma((3,)), dma((3,)), dma((3,)), dma((3,)),
        ],
        compiler_params=pltpu.CompilerParams(
            collective_id=0, has_side_effects=True, vmem_limit_bytes=63 * 1024 * 1024
        ),
        name="span_attention",
    )(hidden_rows, w_query, w_key, w_value, cache_keys, cache_values, key_scale, value_scale, sel_index, sel_count)


def solution(mesh):
    placed = (
        P(("req", "span"), None, None),
        P("span", "head"),
        P("span", "head"),
        P("span", "head"),
        P(("req", "span"), None, "head"),
        P(("req", "span"), None, "head"),
        P(("req", "span"), "head", None),
        P(("req", "span"), "head", None),
        P(("req", "span"), None),
        P(("req", "span")),
    )
    return jax.shard_map(
        shards,
        mesh=mesh,
        in_specs=placed,
        out_specs=(
            P(("req", "span"), None, "head"),
            P(("req", "span"), None, "head"),
            P(("req", "span"), None, "head"),
        ),
        check_vma=False,
    )
```

```python
import functools
import math

import jax
import jax.numpy as jnp
from jax import lax
from jax.experimental import pallas as pl
from jax.experimental.pallas import tpu as pltpu
from jax.sharding import PartitionSpec as P

HEAD_DIM = 128
GROUP = 4
SLOTS = 128
SPAN_LEN = 1024
SIDE = 4
CHIPS = SIDE * SIDE
DEPTH = 256
ROWS = GROUP * SLOTS
KEYS = 2 * SPAN_LEN
EXP2_SCALE = math.log2(math.e) / math.sqrt(HEAD_DIM)
F32 = jnp.float32
BF16 = jnp.bfloat16
OFFSETS = (0, -1, 1, 2)


def position():
    span = lax.axis_index("span")
    core = lax.rem(span, 2)
    chip = lax.div(span, 2)
    return chip, core


def device_of(chip, core):
    return {"span": chip * 2 + core}


class Gather:
    def __init__(self, buf, first, rows, chip, core, send_sem, recv_sem):
        self.buf, self.first, self.rows, self.chip, self.core = buf, first, rows, chip, core
        self.send_sem, self.recv_sem = send_sem, recv_sem
        self.at = (lax.rem(chip, SIDE), lax.div(chip, SIDE))
        self.sent = []

    def block(self, dx, dy):
        x = lax.rem(self.at[0] + (dx + SIDE), SIDE)
        y = lax.rem(self.at[1] + (dy + SIDE), SIDE)
        return y * SIDE + x

    def along(self, axis, first, second):
        return self.block(first, second) if axis == 0 else self.block(second, first)

    def piece(self, half, block, kind):
        size = self.first if half == 0 else self.rows - self.first
        start = half * self.first
        if kind >= 2:
            size //= 2
            start += (kind - 2) * size
        return self.buf.at[block, pl.ds(start, size), :]

    def copy(self, half, stage, j, kind, block, target):
        where = half * 20 + (kind if stage == 1 else 4 + j * 4 + kind)
        ref = self.piece(half, block, kind)
        return pltpu.make_async_remote_copy(
            src_ref=ref,
            dst_ref=ref,
            send_sem=self.send_sem.at[where],
            recv_sem=self.recv_sem.at[where],
            device_id=device_of(target, self.core),
            device_id_type=pl.DeviceIdType.MESH,
        )

    def locate(self, half, stage, j, shift):
        if stage == 1:
            return self.along(half, shift, 0)
        return self.along(half, OFFSETS[j], shift)

    def step(self, half, stage, way):
        axis = half if stage == 1 else 1 - half
        return self.along(axis, way, 0)

    def send(self, half, stage, j, kind, shift):
        way = 1 if kind % 2 == 0 else -1
        one = self.copy(half, stage, j, kind, self.locate(half, stage, j, shift), self.step(half, stage, way))
        one.start()
        self.sent.append(one)

    def receive(self, half, stage, j, kind):
        shift = (-1, 1, 2, 2)[kind]
        self.copy(half, stage, j, kind, self.locate(half, stage, j, shift), self.chip).wait_recv()

    def spread(self, half, stage, j):
        self.send(half, stage, j, 0, 0)
        self.send(half, stage, j, 1, 0)

    def begin(self):
        for half in (0, 1):
            self.spread(half, 1, 0)
        for half in (0, 1):
            self.spread(half, 2, 0)

    def fulls(self, stage, j):
        for kind in (0, 1):
            for half in (0, 1):
                self.receive(half, stage, j, kind)
                self.send(half, stage, j, kind + 2, (-1, 1)[kind])
                if stage == 1:
                    self.spread(half, 2, 1 + kind)

    def quarters(self, stage, j):
        for half in (0, 1):
            for kind in (2, 3):
                self.receive(half, stage, j, kind)
            if stage == 1:
                self.spread(half, 2, 3)

    def finish(self):
        for one in self.sent:
            one.wait_send()


class Ring:
    def __init__(self, refs, whole, at, device, send_sem, recv_sem):
        self.refs, self.whole, self.at, self.device = refs, whole, at, device
        self.send_sem, self.recv_sem = send_sem, recv_sem
        self.sent = []

    def place(self, shift):
        return lax.rem(self.at + (shift + SIDE), SIDE)

    def copy(self, kind, shift, way):
        block = self.place(shift)
        ref = self.whole(block) if kind < 2 else self.refs(block, kind - 2)
        return pltpu.make_async_remote_copy(
            src_ref=ref,
            dst_ref=ref,
            send_sem=self.send_sem.at[kind],
            recv_sem=self.recv_sem.at[kind],
            device_id=self.device(self.place(way)),
            device_id_type=pl.DeviceIdType.MESH,
        )

    def send(self, kind, shift):
        one = self.copy(kind, shift, 1 if kind % 2 == 0 else -1)
        one.start()
        self.sent.append(one)

    def begin(self):
        self.send(0, 0)
        self.send(1, 0)

    def full(self, kind):
        shift = (-1, 1)[kind]
        self.copy(kind, shift, 1).wait_recv()
        self.send(kind + 2, shift)

    def halves(self):
        self.copy(2, 2, 1).wait_recv()
        self.copy(3, 2, 1).wait_recv()

    def finish(self):
        for one in self.sent:
            one.wait_send()


def project(acc, hid_v, buf, block, first=False):
    part = jnp.dot(hid_v[block], buf[block], preferred_element_type=F32)
    acc[...] = part if first else acc[...] + part


def run_gather(gather, acc, hid_v, buf, **hooks):
    def hook(name):
        if name in hooks:
            hooks[name]()

    def work(*pairs):
        for dx, dy in pairs:
            project(acc, hid_v, buf, gather.block(dx, dy))

    hook("start")
    gather.fulls(1, 0)
    hook("one")
    gather.fulls(2, 0)
    hook("two")
    work((-1, 0), (1, 0), (0, -1), (0, 1))
    gather.quarters(1, 0)
    gather.fulls(2, 1)
    hook("three")
    gather.fulls(2, 2)
    hook("four")
    work((-1, -1), (1, -1), (-1, 1), (1, 1))
    gather.quarters(2, 0)
    work((2, 0), (0, 2))
    hook("five")
    gather.fulls(2, 3)
    gather.quarters(2, 1)
    gather.quarters(2, 2)
    work((2, -1), (2, 1), (-1, 2), (1, 2))
    gather.quarters(2, 3)
    hook("six")
    work((2, 2))


def body(
    hid, wq, wk, wv, ck, cv, ks_h, vs_h, sel_h, cnt_h,
    att_o, bk_o, bv_o,
    hid_v, wkv_buf, wq_buf, acc_kv, acc_q, pkv_in, pq_in, cache_v, kv,
    ks, vs, sel, cnt, q_stage, qbuf, peak, mass, accum,
    r_out, r_in, s_out, s_in, fin, att_in,
    local_sem, out_sem, hid_sem, part_sem, sib_send, sib_recv,
    akv_send, akv_recv, aq_send, aq_recv, ring_kv_send, ring_kv_recv, ring_q_send, ring_q_recv,
    sel_send, sel_recv, qy_send, qy_recv, r_send, r_recv, s_send, s_recv, f_send, f_recv,
):
    chip, core = position()
    at_x, at_y = lax.rem(chip, SIDE), lax.div(chip, SIDE)
    sibling = device_of(chip, 1 - core)

    def in_row(x):
        return device_of(at_y * SIDE + x, core)

    def in_column(y):
        return device_of(y * SIDE + at_x, core)

    def remote(src, dst, send_sem, recv_sem, device):
        return pltpu.make_async_remote_copy(
            src_ref=src, dst_ref=dst, send_sem=send_sem, recv_sem=recv_sem,
            device_id=device, device_id_type=pl.DeviceIdType.MESH,
        )

    barrier = pltpu.get_barrier_semaphore()

    def greet(device):
        pl.semaphore_signal(barrier, inc=1, device_id=device, device_id_type=pl.DeviceIdType.MESH)

    greet(sibling)
    for step in (1, 2, 3):
        greet(in_row(lax.rem(at_x + step, SIDE)))
        greet(in_column(lax.rem(at_y + step, SIDE)))

    loads = [
        pltpu.make_async_copy(wk, wkv_buf.at[chip, :, pl.ds(0, HEAD_DIM)], local_sem.at[0]),
        pltpu.make_async_copy(wv, wkv_buf.at[chip, :, pl.ds(HEAD_DIM, HEAD_DIM)], local_sem.at[1]),
        pltpu.make_async_copy(wq, wq_buf.at[chip], local_sem.at[2]),
        pltpu.make_async_copy(ck.at[0], cache_v.at[0], local_sem.at[3]),
        pltpu.make_async_copy(cv.at[0], cache_v.at[1], local_sem.at[4]),
        pltpu.make_async_copy(ks_h, ks, local_sem.at[6]),
        pltpu.make_async_copy(vs_h, vs, local_sem.at[7]),
        pltpu.make_async_copy(sel_h, sel.at[at_y], local_sem.at[8]),
        pltpu.make_async_copy(cnt_h, cnt, local_sem.at[9]),
    ]
    for one in loads:
        one.start()

    def load_hidden(block, carry):
        start = pl.multiple_of((block * 2 + core) * DEPTH, DEPTH)
        pltpu.make_async_copy(
            hid.at[0, :, pl.ds(start, DEPTH)], hid_v.at[block, pl.ds(0, SLOTS), :], local_sem.at[5]
        ).start()
        return carry

    lax.fori_loop(0, CHIPS, load_hidden, 0)
    pl.semaphore_wait(barrier, 7)

    gkv = Gather(wkv_buf, DEPTH // 2, DEPTH, chip, core, akv_send, akv_recv)
    gq = Gather(wq_buf, DEPTH // 4, DEPTH, chip, core, aq_send, aq_recv)
    loads[0].wait()
    loads[1].wait()
    gkv.begin()
    loads[2].wait()

    def send_hidden(block, carry):
        start = pl.multiple_of((block * 2 + 1 - core) * DEPTH, DEPTH)
        remote(
            hid.at[0, :, pl.ds(start, DEPTH)], hid_v.at[block, pl.ds(SLOTS, SLOTS), :],
            hid_sem.at[0], hid_sem.at[1], sibling,
        ).start()
        return carry

    lax.fori_loop(0, CHIPS, send_hidden, 0)
    hid_own = hid_v.at[:, pl.ds(0, SLOTS), :]
    hid_far = hid_v.at[:, pl.ds(SLOTS, SLOTS), :]
    hid_copy = remote(hid_far, hid_far, hid_sem.at[0], hid_sem.at[1], sibling)

    for one in loads[3:]:
        one.wait()

    def column_copy(src, dst, sends, recvs, step, back):
        slot = step - 1
        other = lax.rem(at_y + (SIDE - step if back else step), SIDE)
        return remote(src(other), dst(other if back else at_y), sends.at[slot], recvs.at[slot], in_column(other))

    def sel_copy(step, back):
        return column_copy(
            lambda other: sel.at[other if back else at_y], lambda row: sel.at[row],
            sel_send, sel_recv, step, back,
        )

    for step in (1, 2, 3):
        sel_copy(step, False).start()

    for which, scale in enumerate((ks, vs)):
        for part in range(SPAN_LEN // 128):
            rows = slice(part * 128, (part + 1) * 128)
            spread = jnp.transpose(jnp.broadcast_to(scale[0, :, rows], (128, 128)))
            kv[at_y, which, core, rows, :] = (cache_v[which, rows, :].astype(F32) * spread).astype(BF16)

    def first_kv():
        pltpu.make_async_copy(hid_own, hid_own, local_sem.at[5]).wait()
        hid_copy.wait_recv()
        project(acc_kv, hid_v, wkv_buf, chip, first=True)
        project(acc_q, hid_v, wq_buf, chip, first=True)

    run_gather(gkv, acc_kv, hid_v, wkv_buf, start=first_kv, six=gq.begin)
    kv_part = remote(
        acc_kv.at[pl.ds(SLOTS, SLOTS), :], pkv_in, part_sem.at[0], part_sem.at[1], sibling
    )
    kv_part.start()
    count = cnt[0]
    slot_row = lax.broadcasted_iota(jnp.int32, (1, SLOTS), 1)
    wanted = jnp.where(slot_row < count, sel[at_y], -1)

    rings = [
        Ring(
            lambda row, half, which=which: kv.at[row, which, core, pl.ds(half * 512, 512)],
            lambda row, which=which: kv.at[row, which, core],
            at_y, in_column, ring_kv_send.at[which], ring_kv_recv.at[which],
        )
        for which in (0, 1)
    ]
    ring_q = Ring(
        lambda x, which: qbuf.at[x, pl.ds(which * 2, 2)], lambda x: qbuf.at[x],
        at_x, in_row, ring_q_send, ring_q_recv,
    )

    def to_sibling(which, shift, owner):
        ref = kv.at[rings[which].place(shift), which, owner]
        return remote(ref, ref, sib_send.at[which, shift + 1], sib_recv.at[which, shift + 1], sibling)

    k_out = pltpu.make_async_copy(kv.at[at_y, 0, core], bk_o.at[0], out_sem.at[0])
    v_out = pltpu.make_async_copy(kv.at[at_y, 1, core], bv_o.at[0], out_sem.at[1])

    def blend():
        kv_part.wait_recv()
        fresh = (acc_kv[0:SLOTS, :] + pkv_in[...]).astype(BF16)
        ones = jnp.ones((SLOTS, HEAD_DIM), BF16)

        for step in range(SPAN_LEN // 128):
            here = slice(step * 128, (step + 1) * 128)
            rows = lax.broadcasted_iota(jnp.int32, (128, SLOTS), 0) + step * 128
            chosen = jnp.where(rows == wanted, 1.0, 0.0).astype(BF16)
            moved = jnp.dot(chosen, fresh, preferred_element_type=F32)
            hit = jnp.dot(chosen, ones, preferred_element_type=F32) > 0.5
            for which in (0, 1):
                new = moved[:, which * HEAD_DIM:(which + 1) * HEAD_DIM]
                old = kv[at_y, which, core, here, :].astype(F32)
                kv[at_y, which, core, here, :] = jnp.where(hit, new, old).astype(BF16)

        for which in (0, 1):
            rings[which].begin()
        for which in (0, 1):
            to_sibling(which, 0, core).start()
        k_out.start()
        v_out.start()

    def pass_on(which):
        for kind, shift in ((0, -1), (1, 1)):
            rings[which].full(kind)
            to_sibling(which, shift, core).start()

    def end(which):
        rings[which].halves()
        to_sibling(which, 2, core).start()

    pass_k, pass_v = functools.partial(pass_on, 0), functools.partial(pass_on, 1)
    end_k, end_v = functools.partial(end, 0), functools.partial(end, 1)
    run_gather(gq, acc_q, hid_v, wq_buf, start=blend, two=pass_k, three=pass_v, five=end_k, six=end_v)
    q_part = remote(acc_q.at[pl.ds(SLOTS, SLOTS), :], pq_in, part_sem.at[2], part_sem.at[3], sibling)
    q_part.start()
    peak[...] = jnp.full((SIDE, ROWS, 128), -1e30, F32)
    mass[...] = jnp.zeros((SIDE, ROWS, 128), F32)
    accum[...] = jnp.zeros((SIDE, ROWS, HEAD_DIM), F32)
    q_part.wait_recv()
    for g in range(GROUP):
        cols = slice(g * HEAD_DIM, (g + 1) * HEAD_DIM)
        q_stage[g] = (acc_q[0:SLOTS, cols] + pq_in[:, cols]).astype(BF16)

    def qy_copy(step, back):
        return column_copy(
            lambda other: q_stage.at[other], lambda row: qbuf.at[at_x, row], qy_send, qy_recv, step, back
        )

    for step in (1, 2, 3):
        qy_copy(step, False).start()
    qbuf[at_x, at_y] = q_stage[at_y]
    for step in (1, 2, 3):
        qy_copy(step, True).wait_recv()
        sel_copy(step, True).wait_recv()
    ring_q.begin()
    for shift in (0, -1, 1, 2):
        for which in (0, 1):
            to_sibling(which, shift, 1 - core).wait_recv()

    def scored(x, row, block):
        keys = kv[block, 0].reshape(KEYS, HEAD_DIM)
        return lax.dot_general(
            qbuf[x, row], keys, (((1,), (1,)), ((), ())), preferred_element_type=F32
        )

    def attend(x, pairs, masked):
        ahead = scored(x, *pairs[0])
        for index, (row, block) in enumerate(pairs):
            here = slice(row * SLOTS, (row + 1) * SLOTS)
            scores = ahead
            if index + 1 < len(pairs):
                ahead = scored(x, *pairs[index + 1])
            if masked:
                key = lax.broadcasted_iota(jnp.int32, (SLOTS, KEYS), 1)
                place = jnp.transpose(jnp.broadcast_to(sel[row], (128, 128)))[:, 0:1] + core * SPAN_LEN
                scores = jnp.where(key <= place, scores, -1e30)
            before = peak[x, here, :]
            best = jnp.maximum(before, jnp.max(scores, axis=1, keepdims=True))
            fade = jnp.exp2((before - best) * EXP2_SCALE)
            weights = jnp.exp2((scores - best[:, 0:1]) * EXP2_SCALE)
            peak[x, here, :] = best
            mass[x, here, :] = mass[x, here, :] * fade + jnp.sum(weights, axis=1, keepdims=True)
            accum[x, here, :] = accum[x, here, :] * fade + jnp.dot(
                weights.astype(BF16), kv[block, 1].reshape(KEYS, HEAD_DIM), preferred_element_type=F32
            )

    earlier = [(1, 0), (2, 0), (3, 0), (2, 1), (3, 1), (3, 2)]
    level = [(0, 0), (1, 1), (2, 2), (3, 3)]

    def r_copy(step, back):
        slot = step - 1
        other = lax.rem(at_x + (SIDE - step if back else step), SIDE)
        return (
            remote(
                r_out.at[other], r_in.at[other if back else at_x],
                r_send.at[slot], r_recv.at[slot], in_row(other),
            ),
            remote(
                s_out.at[other], s_in.at[other if back else at_x],
                s_send.at[slot], s_recv.at[slot], in_row(other),
            ),
        )

    def stats(x):
        lane = lax.broadcasted_iota(jnp.int32, (ROWS, 128), 1)
        both = jnp.where(lane == 0, peak[x], mass[x])
        return jnp.transpose(both)[0:8, :]

    def one_chip(index, carry):
        step = jnp.where(index == 0, 0, jnp.where(index == 1, 3, jnp.where(index == 2, 2, 1)))
        x = lax.rem(at_x + step, SIDE)

        @pl.when(index == 1)
        def _():
            ring_q.full(0)
            ring_q.full(1)

        @pl.when(index == 2)
        def _():
            ring_q.halves()

        attend(x, earlier, False)

        @pl.when(x > at_x)
        def _():
            attend(x, level, False)

        @pl.when(index > 0)
        def _():
            r_out[x] = accum[x].astype(BF16)
            s_out[x] = stats(x)

        for which, way in ((1, 3), (2, 2), (3, 1)):
            @pl.when(index == which)
            def _(way=way):
                for one in r_copy(way, False):
                    one.start()

        return carry

    lax.fori_loop(0, SIDE, one_chip, 0)
    attend(at_x, level, True)
    s_in[at_x] = stats(at_x)
    for step in (1, 3, 2):
        for one in r_copy(step, True):
            one.wait_recv()
    seen = s_in[...]
    bests = seen[:, 0:1, :]
    top = jnp.max(bests, axis=0, keepdims=True)
    factor = jnp.exp2((bests - top) * EXP2_SCALE)
    total = jnp.sum(factor * seen[:, 1:2, :], axis=0, keepdims=True)
    factor = jnp.broadcast_to(factor / total, (SIDE, 32, ROWS)).reshape(SIDE * 32, ROWS)
    factor = jnp.transpose(factor)
    r_in[at_x] = accum[at_x].astype(BF16)
    merged = jnp.zeros((ROWS, HEAD_DIM), F32)
    for x in range(SIDE):
        merged += r_in[x].astype(F32) * factor[:, x * 32:x * 32 + 1]
    fin[...] = merged.reshape(SIDE, SLOTS, HEAD_DIM).astype(BF16)

    def f_copy(step, back):
        return column_copy(
            lambda other: fin.at[other], lambda row: att_in.at[row], f_send, f_recv, step, back
        )

    for step in (1, 2, 3):
        f_copy(step, False).start()
    att_in[at_y] = fin[at_y]
    for step in (1, 2, 3):
        f_copy(step, True).wait_recv()
    used = lax.broadcasted_iota(jnp.int32, (SLOTS, HEAD_DIM), 0) < count
    for g in range(GROUP):
        cols = slice(g * HEAD_DIM, (g + 1) * HEAD_DIM)
        att_o[0, :, cols] = jnp.where(used, att_in[g].astype(F32), 0.0).astype(BF16)

    gkv.finish()
    gq.finish()
    for one in rings:
        one.finish()
    for kind in range(4):
        ring_q.copy(kind, 0, 1).wait_send()
    hid_copy.wait_send()
    kv_part.wait_send()
    q_part.wait_send()
    for shift in (0, -1, 1, 2):
        for which in (0, 1):
            to_sibling(which, shift, core).wait_send()
    for step in (1, 2, 3):
        sel_copy(step, False).wait_send()
        qy_copy(step, False).wait_send()
        f_copy(step, False).wait_send()
        for one in r_copy(step, False):
            one.wait_send()
    for one in (k_out, v_out):
        one.wait()


def shards(hidden_rows, w_query, w_key, w_value, cache_keys, cache_values, key_scale, value_scale, sel_index, sel_count):
    hbm_spec = pl.BlockSpec(memory_space=pltpu.HBM)
    dma = pltpu.SemaphoreType.DMA
    return pl.pallas_call(
        body,
        out_shape=(
            pltpu.VMEM((1, SLOTS, ROWS), BF16),
            pltpu.VMEM((1, SPAN_LEN, HEAD_DIM), BF16),
            pltpu.VMEM((1, SPAN_LEN, HEAD_DIM), BF16),
        ),
        in_specs=[hbm_spec] * 10,
        out_specs=(pl.BlockSpec(memory_space=pltpu.VMEM),) * 3,
        scratch_shapes=[
            pltpu.VMEM((CHIPS, 2 * SLOTS, DEPTH), BF16),
            pltpu.VMEM((CHIPS, DEPTH, 2 * HEAD_DIM), BF16),
            pltpu.VMEM((CHIPS, DEPTH, ROWS), BF16),
            pltpu.VMEM((2 * SLOTS, 2 * HEAD_DIM), F32),
            pltpu.VMEM((2 * SLOTS, ROWS), F32),
            pltpu.VMEM((SLOTS, 2 * HEAD_DIM), F32),
            pltpu.VMEM((SLOTS, ROWS), F32),
            pltpu.VMEM((2, SPAN_LEN, HEAD_DIM), BF16),
            pltpu.VMEM((SIDE, 2, 2, SPAN_LEN, HEAD_DIM), BF16),
            pltpu.VMEM((1, 1, SPAN_LEN), F32),
            pltpu.VMEM((1, 1, SPAN_LEN), F32),
            pltpu.VMEM((SIDE, 1, SLOTS), jnp.int32),
            pltpu.SMEM((1,), jnp.int32),
            pltpu.VMEM((GROUP, SLOTS, HEAD_DIM), BF16),
            pltpu.VMEM((SIDE, SIDE, SLOTS, HEAD_DIM), BF16),
            pltpu.VMEM((SIDE, ROWS, 128), F32),
            pltpu.VMEM((SIDE, ROWS, 128), F32),
            pltpu.VMEM((SIDE, ROWS, HEAD_DIM), F32),
            pltpu.VMEM((SIDE, ROWS, HEAD_DIM), BF16),
            pltpu.VMEM((SIDE, ROWS, HEAD_DIM), BF16),
            pltpu.VMEM((SIDE, 8, ROWS), F32),
            pltpu.VMEM((SIDE, 8, ROWS), F32),
            pltpu.VMEM((SIDE, SLOTS, HEAD_DIM), BF16),
            pltpu.VMEM((SIDE, SLOTS, HEAD_DIM), BF16),
            dma((10,)), dma((2,)), dma((2,)), dma((4,)), dma((2, 4)), dma((2, 4)),
            dma((40,)), dma((40,)), dma((40,)), dma((40,)), dma((2, 4)), dma((2, 4)), dma((4,)), dma((4,)),
            dma((3,)), dma((3,)), dma((3,)), dma((3,)), dma((3,)), dma((3,)), dma((3,)), dma((3,)), dma((3,)), dma((3,)),
        ],
        compiler_params=pltpu.CompilerParams(
            collective_id=0, has_side_effects=True, vmem_limit_bytes=63 * 1024 * 1024
        ),
        name="span_attention",
    )(hidden_rows, w_query, w_key, w_value, cache_keys, cache_values, key_scale, value_scale, sel_index, sel_count)


def solution(mesh):
    placed = (
        P(("req", "span"), None, None),
        P("span", "head"),
        P("span", "head"),
        P("span", "head"),
        P(("req", "span"), None, "head"),
        P(("req", "span"), None, "head"),
        P(("req", "span"), "head", None),
        P(("req", "span"), "head", None),
        P(("req", "span"), None),
        P(("req", "span")),
    )
    return jax.shard_map(
        shards,
        mesh=mesh,
        in_specs=placed,
        out_specs=(
            P(("req", "span"), None, "head"),
            P(("req", "span"), None, "head"),
            P(("req", "span"), None, "head"),
        ),
        check_vma=False,
    )
```

```python
import functools
import math

import jax
import jax.numpy as jnp
from jax import lax
from jax.experimental import pallas as pl
from jax.experimental.pallas import tpu as pltpu
from jax.sharding import PartitionSpec as P

HEAD_DIM = 128
GROUP = 4
SLOTS = 128
SPAN_LEN = 1024
SIDE = 4
CHIPS = SIDE * SIDE
DEPTH = 256
ROWS = GROUP * SLOTS
KEYS = 2 * SPAN_LEN
EXP2_SCALE = math.log2(math.e) / math.sqrt(HEAD_DIM)
F32 = jnp.float32
BF16 = jnp.bfloat16
OFFSETS = (0, -1, 1, 2)


def position():
    span = lax.axis_index("span")
    core = lax.rem(span, 2)
    chip = lax.div(span, 2)
    return chip, core


def device_of(chip, core):
    return {"span": chip * 2 + core}


class Gather:
    def __init__(self, buf, first, rows, chip, core, send_sem, recv_sem):
        self.buf, self.first, self.rows, self.chip, self.core = buf, first, rows, chip, core
        self.send_sem, self.recv_sem = send_sem, recv_sem
        self.at = (lax.rem(chip, SIDE), lax.div(chip, SIDE))
        self.sent = []

    def block(self, dx, dy):
        x = lax.rem(self.at[0] + (dx + SIDE), SIDE)
        y = lax.rem(self.at[1] + (dy + SIDE), SIDE)
        return y * SIDE + x

    def along(self, axis, first, second):
        return self.block(first, second) if axis == 0 else self.block(second, first)

    def piece(self, half, block, kind):
        size = self.first if half == 0 else self.rows - self.first
        start = half * self.first
        if kind >= 2:
            size //= 2
            start += (kind - 2) * size
        return self.buf.at[block, pl.ds(start, size), :]

    def copy(self, half, stage, j, kind, block, target):
        where = half * 20 + (kind if stage == 1 else 4 + j * 4 + kind)
        ref = self.piece(half, block, kind)
        return pltpu.make_async_remote_copy(
            src_ref=ref,
            dst_ref=ref,
            send_sem=self.send_sem.at[where],
            recv_sem=self.recv_sem.at[where],
            device_id=device_of(target, self.core),
            device_id_type=pl.DeviceIdType.MESH,
        )

    def locate(self, half, stage, j, shift):
        if stage == 1:
            return self.along(half, shift, 0)
        return self.along(half, OFFSETS[j], shift)

    def step(self, half, stage, way):
        axis = half if stage == 1 else 1 - half
        return self.along(axis, way, 0)

    def send(self, half, stage, j, kind, shift):
        way = 1 if kind % 2 == 0 else -1
        one = self.copy(half, stage, j, kind, self.locate(half, stage, j, shift), self.step(half, stage, way))
        one.start()
        self.sent.append(one)

    def receive(self, half, stage, j, kind):
        shift = (-1, 1, 2, 2)[kind]
        self.copy(half, stage, j, kind, self.locate(half, stage, j, shift), self.chip).wait_recv()

    def spread(self, half, stage, j):
        self.send(half, stage, j, 0, 0)
        self.send(half, stage, j, 1, 0)

    def begin(self):
        for half in (0, 1):
            self.spread(half, 1, 0)
        for half in (0, 1):
            self.spread(half, 2, 0)

    def fulls(self, stage, j):
        for kind in (0, 1):
            for half in (0, 1):
                self.receive(half, stage, j, kind)
                self.send(half, stage, j, kind + 2, (-1, 1)[kind])
                if stage == 1:
                    self.spread(half, 2, 1 + kind)

    def quarters(self, stage, j):
        for half in (0, 1):
            for kind in (2, 3):
                self.receive(half, stage, j, kind)
            if stage == 1:
                self.spread(half, 2, 3)

    def finish(self):
        for one in self.sent:
            one.wait_send()


class Ring:
    def __init__(self, refs, whole, at, device, send_sem, recv_sem):
        self.refs, self.whole, self.at, self.device = refs, whole, at, device
        self.send_sem, self.recv_sem = send_sem, recv_sem
        self.sent = []

    def place(self, shift):
        return lax.rem(self.at + (shift + SIDE), SIDE)

    def copy(self, kind, shift, way):
        block = self.place(shift)
        ref = self.whole(block) if kind < 2 else self.refs(block, kind - 2)
        return pltpu.make_async_remote_copy(
            src_ref=ref,
            dst_ref=ref,
            send_sem=self.send_sem.at[kind],
            recv_sem=self.recv_sem.at[kind],
            device_id=self.device(self.place(way)),
            device_id_type=pl.DeviceIdType.MESH,
        )

    def send(self, kind, shift):
        one = self.copy(kind, shift, 1 if kind % 2 == 0 else -1)
        one.start()
        self.sent.append(one)

    def begin(self):
        self.send(0, 0)
        self.send(1, 0)

    def full(self, kind):
        shift = (-1, 1)[kind]
        self.copy(kind, shift, 1).wait_recv()
        self.send(kind + 2, shift)

    def halves(self):
        self.copy(2, 2, 1).wait_recv()
        self.copy(3, 2, 1).wait_recv()

    def finish(self):
        for one in self.sent:
            one.wait_send()


def project(acc, hid_v, buf, block, first=False):
    part = jnp.dot(hid_v[block], buf[block], preferred_element_type=F32)
    acc[...] = part if first else acc[...] + part


def run_gather(gather, acc, hid_v, buf, **hooks):
    def hook(name):
        if name in hooks:
            hooks[name]()

    def work(*pairs):
        for dx, dy in pairs:
            project(acc, hid_v, buf, gather.block(dx, dy))

    hook("start")
    gather.fulls(1, 0)
    hook("one")
    gather.fulls(2, 0)
    hook("two")
    work((-1, 0), (1, 0), (0, -1), (0, 1))
    gather.quarters(1, 0)
    gather.fulls(2, 1)
    hook("three")
    gather.fulls(2, 2)
    hook("four")
    work((-1, -1), (1, -1), (-1, 1), (1, 1))
    gather.quarters(2, 0)
    work((2, 0), (0, 2))
    hook("five")
    gather.fulls(2, 3)
    gather.quarters(2, 1)
    gather.quarters(2, 2)
    work((2, -1), (2, 1), (-1, 2), (1, 2))
    gather.quarters(2, 3)
    hook("six")
    work((2, 2))


def body(
    hid, wq, wk, wv, ck, cv, ks_h, vs_h, sel_h, cnt_h,
    att_o, bk_o, bv_o,
    hid_v, wkv_buf, wq_buf, acc_kv, acc_q, pkv_in, pq_in, cache_v, kv,
    ks, vs, sel, cnt, q_stage, qbuf, peak, mass, accum,
    r_out, r_in, s_out, s_in, fin, att_in,
    local_sem, out_sem, hid_sem, part_sem, sib_send, sib_recv,
    akv_send, akv_recv, aq_send, aq_recv, ring_kv_send, ring_kv_recv, ring_q_send, ring_q_recv,
    sel_send, sel_recv, qy_send, qy_recv, r_send, r_recv, s_send, s_recv, f_send, f_recv,
):
    chip, core = position()
    at_x, at_y = lax.rem(chip, SIDE), lax.div(chip, SIDE)
    sibling = device_of(chip, 1 - core)

    def in_row(x):
        return device_of(at_y * SIDE + x, core)

    def in_column(y):
        return device_of(y * SIDE + at_x, core)

    def remote(src, dst, send_sem, recv_sem, device):
        return pltpu.make_async_remote_copy(
            src_ref=src, dst_ref=dst, send_sem=send_sem, recv_sem=recv_sem,
            device_id=device, device_id_type=pl.DeviceIdType.MESH,
        )

    barrier = pltpu.get_barrier_semaphore()

    def greet(device):
        pl.semaphore_signal(barrier, inc=1, device_id=device, device_id_type=pl.DeviceIdType.MESH)

    greet(sibling)
    for step in (1, 2, 3):
        greet(in_row(lax.rem(at_x + step, SIDE)))
        greet(in_column(lax.rem(at_y + step, SIDE)))

    loads = [
        pltpu.make_async_copy(wk, wkv_buf.at[chip, :, pl.ds(0, HEAD_DIM)], local_sem.at[0]),
        pltpu.make_async_copy(wv, wkv_buf.at[chip, :, pl.ds(HEAD_DIM, HEAD_DIM)], local_sem.at[1]),
        pltpu.make_async_copy(wq, wq_buf.at[chip], local_sem.at[2]),
        pltpu.make_async_copy(ck.at[0], cache_v.at[0], local_sem.at[3]),
        pltpu.make_async_copy(cv.at[0], cache_v.at[1], local_sem.at[4]),
        pltpu.make_async_copy(ks_h, ks, local_sem.at[6]),
        pltpu.make_async_copy(vs_h, vs, local_sem.at[7]),
        pltpu.make_async_copy(sel_h, sel.at[at_y], local_sem.at[8]),
        pltpu.make_async_copy(cnt_h, cnt, local_sem.at[9]),
    ]
    for one in loads:
        one.start()

    def load_hidden(block, carry):
        start = pl.multiple_of((block * 2 + core) * DEPTH, DEPTH)
        pltpu.make_async_copy(
            hid.at[0, :, pl.ds(start, DEPTH)], hid_v.at[block, pl.ds(0, SLOTS), :], local_sem.at[5]
        ).start()
        return carry

    lax.fori_loop(0, CHIPS, load_hidden, 0)
    pl.semaphore_wait(barrier, 7)

    gkv = Gather(wkv_buf, DEPTH // 2, DEPTH, chip, core, akv_send, akv_recv)
    gq = Gather(wq_buf, DEPTH // 4, DEPTH, chip, core, aq_send, aq_recv)
    loads[0].wait()
    loads[1].wait()
    gkv.begin()
    loads[2].wait()

    def send_hidden(block, carry):
        start = pl.multiple_of((block * 2 + 1 - core) * DEPTH, DEPTH)
        remote(
            hid.at[0, :, pl.ds(start, DEPTH)], hid_v.at[block, pl.ds(SLOTS, SLOTS), :],
            hid_sem.at[0], hid_sem.at[1], sibling,
        ).start()
        return carry

    lax.fori_loop(0, CHIPS, send_hidden, 0)
    hid_own = hid_v.at[:, pl.ds(0, SLOTS), :]
    hid_far = hid_v.at[:, pl.ds(SLOTS, SLOTS), :]
    hid_copy = remote(hid_far, hid_far, hid_sem.at[0], hid_sem.at[1], sibling)

    for one in loads[3:]:
        one.wait()

    def column_copy(src, dst, sends, recvs, step, back):
        slot = step - 1
        other = lax.rem(at_y + (SIDE - step if back else step), SIDE)
        return remote(src(other), dst(other if back else at_y), sends.at[slot], recvs.at[slot], in_column(other))

    def sel_copy(step, back):
        return column_copy(
            lambda other: sel.at[other if back else at_y], lambda row: sel.at[row],
            sel_send, sel_recv, step, back,
        )

    for step in (1, 2, 3):
        sel_copy(step, False).start()

    def dequantize():
        for which, scale in enumerate((ks, vs)):
            for part in range(SPAN_LEN // 128):
                rows = slice(part * 128, (part + 1) * 128)
                spread = jnp.transpose(jnp.broadcast_to(scale[0, :, rows], (128, 128)))
                kv[at_y, which, core, rows, :] = (cache_v[which, rows, :].astype(F32) * spread).astype(BF16)

    def first_kv():
        pltpu.make_async_copy(hid_own, hid_own, local_sem.at[5]).wait()
        hid_copy.wait_recv()
        project(acc_kv, hid_v, wkv_buf, chip, first=True)
        project(acc_q, hid_v, wq_buf, chip, first=True)

    run_gather(gkv, acc_kv, hid_v, wkv_buf, two=first_kv, four=dequantize, six=gq.begin)
    kv_part = remote(
        acc_kv.at[pl.ds(SLOTS, SLOTS), :], pkv_in, part_sem.at[0], part_sem.at[1], sibling
    )
    kv_part.start()
    count = cnt[0]
    slot_row = lax.broadcasted_iota(jnp.int32, (1, SLOTS), 1)
    wanted = jnp.where(slot_row < count, sel[at_y], -1)

    rings = [
        Ring(
            lambda row, half, which=which: kv.at[row, which, core, pl.ds(half * 512, 512)],
            lambda row, which=which: kv.at[row, which, core],
            at_y, in_column, ring_kv_send.at[which], ring_kv_recv.at[which],
        )
        for which in (0, 1)
    ]
    ring_q = Ring(
        lambda x, which: qbuf.at[x, pl.ds(which * 2, 2)], lambda x: qbuf.at[x],
        at_x, in_row, ring_q_send, ring_q_recv,
    )

    def to_sibling(which, shift, owner):
        ref = kv.at[rings[which].place(shift), which, owner]
        return remote(ref, ref, sib_send.at[which, shift + 1], sib_recv.at[which, shift + 1], sibling)

    k_out = pltpu.make_async_copy(kv.at[at_y, 0, core], bk_o.at[0], out_sem.at[0])
    v_out = pltpu.make_async_copy(kv.at[at_y, 1, core], bv_o.at[0], out_sem.at[1])

    def blend():
        kv_part.wait_recv()
        fresh = (acc_kv[0:SLOTS, :] + pkv_in[...]).astype(BF16)
        ones = jnp.ones((SLOTS, HEAD_DIM), BF16)

        for step in range(SPAN_LEN // 128):
            here = slice(step * 128, (step + 1) * 128)
            rows = lax.broadcasted_iota(jnp.int32, (128, SLOTS), 0) + step * 128
            chosen = jnp.where(rows == wanted, 1.0, 0.0).astype(BF16)
            moved = jnp.dot(chosen, fresh, preferred_element_type=F32)
            hit = jnp.dot(chosen, ones, preferred_element_type=F32) > 0.5
            for which in (0, 1):
                new = moved[:, which * HEAD_DIM:(which + 1) * HEAD_DIM]
                old = kv[at_y, which, core, here, :].astype(F32)
                kv[at_y, which, core, here, :] = jnp.where(hit, new, old).astype(BF16)

        for which in (0, 1):
            rings[which].begin()
        for which in (0, 1):
            to_sibling(which, 0, core).start()
        k_out.start()
        v_out.start()

    def pass_on(which):
        for kind, shift in ((0, -1), (1, 1)):
            rings[which].full(kind)
            to_sibling(which, shift, core).start()

    def end(which):
        rings[which].halves()
        to_sibling(which, 2, core).start()

    pass_k, pass_v = functools.partial(pass_on, 0), functools.partial(pass_on, 1)
    end_k, end_v = functools.partial(end, 0), functools.partial(end, 1)
    run_gather(gq, acc_q, hid_v, wq_buf, start=blend, two=pass_k, three=pass_v, five=end_k, six=end_v)
    q_part = remote(acc_q.at[pl.ds(SLOTS, SLOTS), :], pq_in, part_sem.at[2], part_sem.at[3], sibling)
    q_part.start()
    peak[...] = jnp.full((SIDE, ROWS, 128), -1e30, F32)
    mass[...] = jnp.zeros((SIDE, ROWS, 128), F32)
    accum[...] = jnp.zeros((SIDE, ROWS, HEAD_DIM), F32)
    q_part.wait_recv()
    for g in range(GROUP):
        cols = slice(g * HEAD_DIM, (g + 1) * HEAD_DIM)
        q_stage[g] = (acc_q[0:SLOTS, cols] + pq_in[:, cols]).astype(BF16)

    def qy_copy(step, back):
        return column_copy(
            lambda other: q_stage.at[other], lambda row: qbuf.at[at_x, row], qy_send, qy_recv, step, back
        )

    for step in (1, 2, 3):
        qy_copy(step, False).start()
    qbuf[at_x, at_y] = q_stage[at_y]
    for step in (1, 2, 3):
        qy_copy(step, True).wait_recv()
        sel_copy(step, True).wait_recv()
    ring_q.begin()
    for shift in (0, -1, 1, 2):
        for which in (0, 1):
            to_sibling(which, shift, 1 - core).wait_recv()

    def scored(x, row, block):
        keys = kv[block, 0].reshape(KEYS, HEAD_DIM)
        return lax.dot_general(
            qbuf[x, row], keys, (((1,), (1,)), ((), ())), preferred_element_type=F32
        )

    def attend(x, pairs, masked):
        ahead = scored(x, *pairs[0])
        for index, (row, block) in enumerate(pairs):
            here = slice(row * SLOTS, (row + 1) * SLOTS)
            scores = ahead
            if index + 1 < len(pairs):
                ahead = scored(x, *pairs[index + 1])
            if masked:
                key = lax.broadcasted_iota(jnp.int32, (SLOTS, KEYS), 1)
                place = jnp.transpose(jnp.broadcast_to(sel[row], (128, 128)))[:, 0:1] + core * SPAN_LEN
                scores = jnp.where(key <= place, scores, -1e30)
            before = peak[x, here, :]
            best = jnp.maximum(before, jnp.max(scores, axis=1, keepdims=True))
            fade = jnp.exp2((before - best) * EXP2_SCALE)
            weights = jnp.exp2((scores - best[:, 0:1]) * EXP2_SCALE)
            peak[x, here, :] = best
            mass[x, here, :] = mass[x, here, :] * fade + jnp.sum(weights, axis=1, keepdims=True)
            accum[x, here, :] = accum[x, here, :] * fade + jnp.dot(
                weights.astype(BF16), kv[block, 1].reshape(KEYS, HEAD_DIM), preferred_element_type=F32
            )

    earlier = [(1, 0), (2, 0), (3, 0), (2, 1), (3, 1), (3, 2)]
    level = [(0, 0), (1, 1), (2, 2), (3, 3)]

    def r_copy(step, back):
        slot = step - 1
        other = lax.rem(at_x + (SIDE - step if back else step), SIDE)
        return (
            remote(
                r_out.at[other], r_in.at[other if back else at_x],
                r_send.at[slot], r_recv.at[slot], in_row(other),
            ),
            remote(
                s_out.at[other], s_in.at[other if back else at_x],
                s_send.at[slot], s_recv.at[slot], in_row(other),
            ),
        )

    def stats(x):
        lane = lax.broadcasted_iota(jnp.int32, (ROWS, 128), 1)
        both = jnp.where(lane == 0, peak[x], mass[x])
        return jnp.transpose(both)[0:8, :]

    def one_chip(index, carry):
        step = jnp.where(index == 0, 0, jnp.where(index == 1, 3, jnp.where(index == 2, 2, 1)))
        x = lax.rem(at_x + step, SIDE)

        @pl.when(index == 1)
        def _():
            ring_q.full(0)
            ring_q.full(1)

        @pl.when(index == 2)
        def _():
            ring_q.halves()

        attend(x, earlier, False)

        @pl.when(x > at_x)
        def _():
            attend(x, level, False)

        @pl.when(index > 0)
        def _():
            r_out[x] = accum[x].astype(BF16)
            s_out[x] = stats(x)

        for which, way in ((1, 3), (2, 2), (3, 1)):
            @pl.when(index == which)
            def _(way=way):
                for one in r_copy(way, False):
                    one.start()

        return carry

    lax.fori_loop(0, SIDE, one_chip, 0)
    attend(at_x, level, True)
    s_in[at_x] = stats(at_x)
    for step in (1, 3, 2):
        for one in r_copy(step, True):
            one.wait_recv()
    seen = s_in[...]
    bests = seen[:, 0:1, :]
    top = jnp.max(bests, axis=0, keepdims=True)
    factor = jnp.exp2((bests - top) * EXP2_SCALE)
    total = jnp.sum(factor * seen[:, 1:2, :], axis=0, keepdims=True)
    factor = jnp.broadcast_to(factor / total, (SIDE, 32, ROWS)).reshape(SIDE * 32, ROWS)
    factor = jnp.transpose(factor)
    r_in[at_x] = accum[at_x].astype(BF16)
    merged = jnp.zeros((ROWS, HEAD_DIM), F32)
    for x in range(SIDE):
        merged += r_in[x].astype(F32) * factor[:, x * 32:x * 32 + 1]
    fin[...] = merged.reshape(SIDE, SLOTS, HEAD_DIM).astype(BF16)

    def f_copy(step, back):
        return column_copy(
            lambda other: fin.at[other], lambda row: att_in.at[row], f_send, f_recv, step, back
        )

    for step in (1, 2, 3):
        f_copy(step, False).start()
    att_in[at_y] = fin[at_y]
    for step in (1, 2, 3):
        f_copy(step, True).wait_recv()
    used = lax.broadcasted_iota(jnp.int32, (SLOTS, HEAD_DIM), 0) < count
    for g in range(GROUP):
        cols = slice(g * HEAD_DIM, (g + 1) * HEAD_DIM)
        att_o[0, :, cols] = jnp.where(used, att_in[g].astype(F32), 0.0).astype(BF16)

    gkv.finish()
    gq.finish()
    for one in rings:
        one.finish()
    for kind in range(4):
        ring_q.copy(kind, 0, 1).wait_send()
    hid_copy.wait_send()
    kv_part.wait_send()
    q_part.wait_send()
    for shift in (0, -1, 1, 2):
        for which in (0, 1):
            to_sibling(which, shift, core).wait_send()
    for step in (1, 2, 3):
        sel_copy(step, False).wait_send()
        qy_copy(step, False).wait_send()
        f_copy(step, False).wait_send()
        for one in r_copy(step, False):
            one.wait_send()
    for one in (k_out, v_out):
        one.wait()


def shards(hidden_rows, w_query, w_key, w_value, cache_keys, cache_values, key_scale, value_scale, sel_index, sel_count):
    hbm_spec = pl.BlockSpec(memory_space=pltpu.HBM)
    dma = pltpu.SemaphoreType.DMA
    return pl.pallas_call(
        body,
        out_shape=(
            pltpu.VMEM((1, SLOTS, ROWS), BF16),
            pltpu.VMEM((1, SPAN_LEN, HEAD_DIM), BF16),
            pltpu.VMEM((1, SPAN_LEN, HEAD_DIM), BF16),
        ),
        in_specs=[hbm_spec] * 10,
        out_specs=(pl.BlockSpec(memory_space=pltpu.VMEM),) * 3,
        scratch_shapes=[
            pltpu.VMEM((CHIPS, 2 * SLOTS, DEPTH), BF16),
            pltpu.VMEM((CHIPS, DEPTH, 2 * HEAD_DIM), BF16),
            pltpu.VMEM((CHIPS, DEPTH, ROWS), BF16),
            pltpu.VMEM((2 * SLOTS, 2 * HEAD_DIM), F32),
            pltpu.VMEM((2 * SLOTS, ROWS), F32),
            pltpu.VMEM((SLOTS, 2 * HEAD_DIM), F32),
            pltpu.VMEM((SLOTS, ROWS), F32),
            pltpu.VMEM((2, SPAN_LEN, HEAD_DIM), BF16),
            pltpu.VMEM((SIDE, 2, 2, SPAN_LEN, HEAD_DIM), BF16),
            pltpu.VMEM((1, 1, SPAN_LEN), F32),
            pltpu.VMEM((1, 1, SPAN_LEN), F32),
            pltpu.VMEM((SIDE, 1, SLOTS), jnp.int32),
            pltpu.SMEM((1,), jnp.int32),
            pltpu.VMEM((GROUP, SLOTS, HEAD_DIM), BF16),
            pltpu.VMEM((SIDE, SIDE, SLOTS, HEAD_DIM), BF16),
            pltpu.VMEM((SIDE, ROWS, 128), F32),
            pltpu.VMEM((SIDE, ROWS, 128), F32),
            pltpu.VMEM((SIDE, ROWS, HEAD_DIM), F32),
            pltpu.VMEM((SIDE, ROWS, HEAD_DIM), BF16),
            pltpu.VMEM((SIDE, ROWS, HEAD_DIM), BF16),
            pltpu.VMEM((SIDE, 8, ROWS), F32),
            pltpu.VMEM((SIDE, 8, ROWS), F32),
            pltpu.VMEM((SIDE, SLOTS, HEAD_DIM), BF16),
            pltpu.VMEM((SIDE, SLOTS, HEAD_DIM), BF16),
            dma((10,)), dma((2,)), dma((2,)), dma((4,)), dma((2, 4)), dma((2, 4)),
            dma((40,)), dma((40,)), dma((40,)), dma((40,)), dma((2, 4)), dma((2, 4)), dma((4,)), dma((4,)),
            dma((3,)), dma((3,)), dma((3,)), dma((3,)), dma((3,)), dma((3,)), dma((3,)), dma((3,)), dma((3,)), dma((3,)),
        ],
        compiler_params=pltpu.CompilerParams(
            collective_id=0, has_side_effects=True, vmem_limit_bytes=63 * 1024 * 1024
        ),
        name="span_attention",
    )(hidden_rows, w_query, w_key, w_value, cache_keys, cache_values, key_scale, value_scale, sel_index, sel_count)


def solution(mesh):
    placed = (
        P(("req", "span"), None, None),
        P("span", "head"),
        P("span", "head"),
        P("span", "head"),
        P(("req", "span"), None, "head"),
        P(("req", "span"), None, "head"),
        P(("req", "span"), "head", None),
        P(("req", "span"), "head", None),
        P(("req", "span"), None),
        P(("req", "span")),
    )
    return jax.shard_map(
        shards,
        mesh=mesh,
        in_specs=placed,
        out_specs=(
            P(("req", "span"), None, "head"),
            P(("req", "span"), None, "head"),
            P(("req", "span"), None, "head"),
        ),
        check_vma=False,
    )
```
